32 devices in a mesh: groups: 2 (over x), seq: 4 (over z), expert: 4 (over y, core).
Axes of the slice: x: 2, y: 2, z: 4, core: 2. Of those that a mesh axis runs over, the one named last changes fastest.
Arguments:
- q_lat: bfloat16 [512, 65536], P(('groups', 'seq'), 'expert'), parts along dimension 0, may hold values from -36 to 36
- q_rope: bfloat16 [512, 8192], P(('groups', 'seq'), 'expert'), parts along dimension 0, may hold values from -6 to 6
- cache_lat: bfloat16 [2048, 512], P(('groups', 'seq')), parts along dimension 0, may hold values from -7 to 7
- cache_rope: bfloat16 [2048, 64], P(('groups', 'seq')), parts along dimension 0, may hold values from -8 to 8
- tool_lat: bfloat16 [256, 512], P(('groups', 'seq')), parts along dimension 0, may hold values from -2.5 to 2.5
- tool_rope: bfloat16 [256, 64], P(('groups', 'seq')), parts along dimension 0, may hold values from -8 to 8
- offset: int32 [2], P('groups'), parts along dimension 0, may hold values from 512 to 736
- suf_lat: bfloat16 [512, 512], P(('groups', 'seq')), parts along dimension 0, may hold values from -6 to 6
- suf_rope: bfloat16 [512, 64], P(('groups', 'seq')), parts along dimension 0, may hold values from -8 to 8
- w_uv: bfloat16 [128, 512, 128], P('expert'), may hold values from -1 to 1
- w_out: bfloat16 [16384, 7168], P('expert', 'seq'), may hold values from -0.19921875 to 0.19921875
- resid: bfloat16 [512, 7168], P(('groups', 'expert'), 'seq'), parts along dimension 0, may hold values from -36 to 36
- routes: int32 [512, 2], P(('groups', 'expert')), parts along dimension 0, may hold values from 0 to 3, all different within a row; in each aligned block of 64 rows (0 to 63, 64 to 127, ...) at most 40 rows name the same one
- probs: float32 [512, 2], P(('groups', 'expert')), parts along dimension 0, may hold values from 0.1 to 1
- w_gate: bfloat16 [4, 7168, 1024], P('expert', None, 'seq'), may hold values from -0.0625 to 0.0625
- w_up: bfloat16 [4, 7168, 1024], P('expert', None, 'seq'), may hold values from -0.0625 to 0.0625
- w_down: bfloat16 [4, 1024, 7168], P('expert', 'seq'), may hold values from -0.1875 to 0.1875
Outputs:
- attn_residual: bfloat16 [512, 7168], P(('groups', 'expert'), 'seq'), parts along dimension 0
- expert_mix: bfloat16 [512, 7168], P(('groups', 'expert'), 'seq'), parts along dimension 0
The draws below stay inside these ranges and needn't reach their ends.
There are 2 independent parts, one for each index of `groups`. The reference program is written for one: setup_inputs(seed, part) draws one part's arguments, and reference() takes and returns one part's arrays. A program takes and returns all parts, laid end to end along the dimension named above; an argument that names none is the same for every part. Nothing has to cross between parts.
Inputs may be any that keep to these rules, and one draw needn't show every extreme that they name: `routes`: within the rows of one device of the expert axis (64 rows in a row), no expert is named more than 40 times.
All inputs are finite; a program needn't handle non-finite values.
Results may differ from the reference program's by a relative error of at most 0.03.
Values may be sent and summed in bfloat16 or wider, within the bound.
A program may use at most 128 MiB of HBM per device.

```python
import math
import jax
import jax.numpy as jnp
import numpy as np
from jax import lax

D = 7168
H = 128
LAT = 512
ROPE = 64
VDIM = 128
FF_EXP = 1024
CTX_DEV = 256
TOOL_DEV = 32
SUF = 256
CTX = 1024
TOOL = 128
TE = 64
EXPERTS = 4
TOP = 2
CAP = 40
N_SEQ = 4


def base_latents(key):
    return jnp.clip(jax.random.normal(jax.random.fold_in(key, 101), (CTX, LAT), jnp.float32), -6.0, 6.0)


def draw_cache_lat(key, part):
    latents = base_latents(key)
    return latents.astype(jnp.bfloat16)


def draw_q_lat(key, part):
    queries = jnp.clip(jax.random.normal(jax.random.fold_in(key, 104), (SUF, H * LAT), jnp.float32), -6.0, 6.0)
    return queries.astype(jnp.bfloat16)


def draw_resid(key, part):
    row_scale = jnp.exp(jax.random.uniform(jax.random.fold_in(key, 107), (SUF, 1), jnp.float32, jnp.log(0.3), jnp.log(3.0)))
    rise = jnp.sqrt(3.0) ** (jnp.arange(D, dtype=jnp.float32) / D)
    column_scale = rise * jax.random.uniform(jax.random.fold_in(key, 108), (D,), jnp.float32, 0.6, 1.4)
    values = jnp.clip(jax.random.normal(jax.random.fold_in(key, 109), (SUF, D), jnp.float32), -4.0, 4.0)
    return (0.5 * row_scale * column_scale[None, :] * values).astype(jnp.bfloat16)


def block_levels(key, shape, shards, least, top_value):
    level, own = 1.0, jax.random.fold_in(key, 6)
    for axis_at, parts in shards:
        heights = jnp.exp(jax.random.uniform(jax.random.fold_in(own, axis_at), (parts,), jnp.float32, least / len(shards), top_value / len(shards)))
        level = level * jnp.repeat(heights, shape[axis_at] // parts).reshape([-1 if axis == axis_at else 1 for axis in range(len(shape))])
    return level


def assign_block(stream_key, own, number, rows, number_of, top, limit, slope):
    order = jax.random.permutation(stream_key, number_of)
    crowded, ordinary = portions_of(number_of, rows * top, limit, slope, True), portions_of(number_of, rows * top, limit, slope, False)
    places = jnp.arange(number_of)

    def named(sizes, offset_by):
        used = int((sizes > 0).sum())
        fixed = max(1, used // 4)
        moved = fixed + (places - fixed + offset_by * (used - fixed)) % max(1, number_of - fixed)
        return jnp.zeros((number_of,), jnp.int32).at[order[jnp.where(places < fixed, places, moved)]].set(jnp.asarray(sizes, jnp.int32))

    sizes = jnp.where(number % 4 == 0, named(crowded, number // 4), named(ordinary, number - number // 4 - 1))
    mixed = jax.random.permutation(jax.random.fold_in(own, 3), number_of)
    donor, taker = mixed[0:number_of // 2 * 2:2], mixed[1:number_of // 2 * 2:2]
    room = jnp.minimum(sizes[donor] - 1, limit - sizes[taker]) // 2
    room = jnp.where((donor == order[0]) | (taker == order[0]) | (sizes[taker] == 0), 0, jnp.maximum(room, 0))
    moved = jax.random.randint(jax.random.fold_in(own, 4), (number_of // 2,), 0, 1 << 20) % (room + 1)
    sizes = sizes.at[donor].add(-moved).at[taker].add(moved)
    items = jnp.searchsorted(jnp.cumsum(sizes), jnp.arange(rows * top), side="right").astype(jnp.int32)
    grid = items.reshape(top, rows).T
    grid = grid[jax.random.permutation(jax.random.fold_in(own, 1), rows)]
    offset_by = jax.random.randint(jax.random.fold_in(own, 2), (rows, 1), 0, top)
    return jnp.take_along_axis(grid, (jnp.arange(top)[None, :] + offset_by) % top, axis=1)


def portions_of(number_of, total, most, slope, full):
    weights = [(1 << 20) // math.isqrt(grade ** slope) + 1 for grade in range(1, number_of + 1)]
    largest = most if full else min(most, max(-(-total // number_of), total * weights[0] // sum(weights)))
    least = 1 if total - largest >= number_of - 1 else 0
    given, rest = [largest] + [least] * (number_of - 1), total - largest - least * (number_of - 1)
    while rest > 0:
        free = [i for i in range(1, number_of) if given[i] < largest] or [i for i in range(1, number_of) if given[i] < most]
        whole, remaining = sum([weights[i] for i in free]), rest
        for i in free:
            extra = min(most - given[i], max(1, remaining * weights[i] // whole), rest)
            given[i] = given[i] + extra
            rest = rest - extra
    return np.array(given)


def scatter_about(rng, shape, deviation, most, split=(), kind=jnp.bfloat16):
    factor_of = block_levels(rng, shape, split, -0.22, 0.18) if split else 1.0
    result = jax.random.normal(rng, shape, jnp.float32) * deviation * factor_of
    return jnp.minimum(jnp.maximum(result, -most), most).astype(kind)


def setup_inputs(seed: int = 0, part: int = 0) -> dict:
    arg_keys = jax.random.split(jax.random.key(seed), 18)
    own_keys = jax.random.split(jax.random.fold_in(arg_keys[17], part), 18)
    q_lat = draw_q_lat(jax.random.fold_in(jax.random.fold_in(arg_keys[17], part), 71), part)
    q_rope = scatter_about(own_keys[1], (SUF, H * ROPE), 1.0, 6.0, ((0, 4), (1, 4)))
    cache_lat = draw_cache_lat(jax.random.fold_in(jax.random.fold_in(arg_keys[17], part), 71), part)
    cache_rope = scatter_about(own_keys[3], (CTX, ROPE), (12 * ROPE ** -0.5), 8.0, ((0, 4),))
    tool_lat = scatter_about(own_keys[4], (TOOL, LAT), (10 * LAT ** -0.5), 2.5, ((0, 4),))
    tool_rope = scatter_about(own_keys[5], (TOOL, ROPE), (12 * ROPE ** -0.5), 8.0, ((0, 4),))
    offset = jax.random.randint(own_keys[6], (1,), CTX // 2, CTX // 2 + CTX_DEV - TOOL_DEV + 1).astype(jnp.int32)
    suf_lat = scatter_about(own_keys[7], (SUF, LAT), 1.0, 6.0, ((0, 4),))
    suf_rope = scatter_about(own_keys[8], (SUF, ROPE), (12 * ROPE ** -0.5), 8.0, ((0, 4),))
    w_uv = scatter_about(arg_keys[9], (H, LAT, VDIM), 0.15, 1.0, ((0, 4),))
    w_out = scatter_about(arg_keys[10], (H * VDIM, D), 0.03, 0.19921875, ((0, 4), (1, 4)))
    resid = draw_resid(jax.random.fold_in(jax.random.fold_in(arg_keys[17], part), 71), part)
    routes_keys = jax.random.split(jax.random.fold_in(own_keys[12], 1), SUF // TE)
    routes_turns = jax.random.permutation(jax.random.fold_in(own_keys[12], 3), SUF // TE)
    routes = jax.vmap(lambda own, number: assign_block(jax.random.fold_in(own_keys[12], 2), own, number, TE, EXPERTS, TOP, CAP, 1))(routes_keys, routes_turns).reshape((SUF, TOP))
    probs = jnp.clip(0.1 + 0.9 * jax.random.uniform(own_keys[13], (SUF, TOP), jnp.float32) ** block_levels(own_keys[13], (SUF, TOP), ((0, 4),), -0.2, 0.2), 0.1, 1.0)
    w_gate = scatter_about(arg_keys[14], (EXPERTS, D, FF_EXP), D ** -0.5, 0.0625, ((0, 4), (2, 4)))
    w_up = scatter_about(arg_keys[15], (EXPERTS, D, FF_EXP), D ** -0.5, 0.0625, ((0, 4), (2, 4)))
    w_down = scatter_about(arg_keys[16], (EXPERTS, FF_EXP, D), FF_EXP ** -0.5, 0.1875, ((0, 4), (1, 4)))
    return {"q_lat": q_lat, "q_rope": q_rope, "cache_lat": cache_lat, "cache_rope": cache_rope, "tool_lat": tool_lat, "tool_rope": tool_rope, "offset": offset, "suf_lat": suf_lat, "suf_rope": suf_rope, "w_uv": w_uv, "w_out": w_out, "resid": resid, "routes": routes, "probs": probs, "w_gate": w_gate, "w_up": w_up, "w_down": w_down}


score_scale = 192.0 ** (-0.5)

def insert_tool(cache, tool, offset):
    position = jnp.arange(cache.shape[0], dtype=jnp.int32)
    shifted = position - offset[0]
    inside = (shifted >= 0) & (shifted < tool.shape[0])
    safe = jnp.clip(shifted, 0, tool.shape[0] - 1).astype(jnp.int32)
    return jnp.where(inside[:, None], jnp.take(tool, safe, axis=0), cache)

def reference(q_lat, q_rope, cache_lat, cache_rope, tool_lat, tool_rope, offset, suf_lat, suf_rope, w_uv, w_out, resid, routes, probs, w_gate, w_up, w_down):
    key_lat = jnp.concatenate([insert_tool(cache_lat, tool_lat, offset), suf_lat], axis=0)
    key_rope = jnp.concatenate([insert_tool(cache_rope, tool_rope, offset), suf_rope], axis=0)
    query_pos = jnp.arange(SUF, dtype=jnp.int32)
    key_pos = jnp.arange(CTX + SUF, dtype=jnp.int32)
    visible = (key_pos[None, :] < CTX) | (key_pos[None, :] - CTX <= query_pos[:, None])
    lat_heads = q_lat.reshape(SUF, H, LAT).transpose(1, 0, 2)
    rope_heads = q_rope.reshape(SUF, H, ROPE).transpose(1, 0, 2)

    def one_head(operands):
        query_lat, query_rope, value_proj = operands
        scores = jnp.dot(query_lat, key_lat.T, preferred_element_type=jnp.float32)
        scores = (scores + jnp.dot(query_rope, key_rope.T, preferred_element_type=jnp.float32)) * score_scale
        scores = jnp.where(visible, scores, -jnp.inf)
        highest = lax.optimization_barrier(jnp.max(scores, axis=1, keepdims=True))
        weights = jnp.where(visible, jnp.exp(scores - highest), 0.0)
        total = lax.optimization_barrier(jnp.sum(weights, axis=1, keepdims=True))
        latent_out = (jnp.dot(weights.astype(jnp.bfloat16), key_lat, preferred_element_type=jnp.float32) / total).astype(jnp.bfloat16)
        return jnp.dot(latent_out, value_proj, preferred_element_type=jnp.float32).astype(jnp.bfloat16)
    values = lax.map(one_head, (lat_heads, rope_heads, w_uv))
    values = values.transpose(1, 0, 2).reshape(SUF, H * VDIM)
    attn_residual = (resid.astype(jnp.float32) + jnp.dot(values, w_out, preferred_element_type=jnp.float32)).astype(jnp.bfloat16)
    stream = attn_residual.astype(jnp.float32)
    normed = (stream * lax.rsqrt(lax.optimization_barrier(jnp.mean(stream * stream, axis=1, keepdims=True)) + 1e-06)).astype(jnp.bfloat16)
    route_weight = 2.5 * probs / lax.optimization_barrier(jnp.sum(probs, axis=1, keepdims=True))
    block_units = FF_EXP // N_SEQ

    def one_expert(mixed, operands):
        gate_proj, up_proj, down_proj, expert_id = operands
        gate = jnp.dot(normed, gate_proj, preferred_element_type=jnp.float32)
        upper = jnp.dot(normed, up_proj, preferred_element_type=jnp.float32)
        inner = (jax.nn.silu(gate) * upper).astype(jnp.bfloat16)
        blocks = jnp.einsum('tsf,sfd->tsd', inner.reshape(SUF, N_SEQ, block_units).astype(jnp.float32), down_proj.reshape(N_SEQ, block_units, D).astype(jnp.float32))
        rounded = lax.optimization_barrier(blocks.astype(jnp.bfloat16))
        summed = lax.optimization_barrier(jnp.sum(rounded.astype(jnp.float32), axis=1))
        expert_out = lax.optimization_barrier(summed.astype(jnp.bfloat16)).astype(jnp.float32)
        weight = lax.optimization_barrier(jnp.sum(route_weight * (routes == expert_id).astype(jnp.float32), axis=1))
        return (mixed + weight[:, None] * expert_out, None)
    mixed, unused = lax.scan(one_expert, jnp.zeros((SUF, D), jnp.float32), (w_gate, w_up, w_down, jnp.arange(EXPERTS, dtype=jnp.int32)))
    return (attn_residual, mixed.astype(jnp.bfloat16))
```

```python
import functools

import jax
import jax.numpy as jnp
from jax import lax
from jax.experimental import pallas as pl
from jax.experimental.pallas import tpu as pltpu
from jax.sharding import PartitionSpec as P

MESH = pl.DeviceIdType.MESH
norm_eps = 1e-06
exp2_scale = 192.0 ** (-0.5) * 1.4426950408889634
floor_score = -1e30
lanes = 128


def dot(a, b):
    return jnp.dot(a, b, preferred_element_type=jnp.float32)


def dot_nt(a, b):
    return lax.dot_general(a, b, (((1,), (1,)), ((), ())), preferred_element_type=jnp.float32)


def column_tile(width):
    return 256 if width % 256 == 0 else 128


def layer_kernel(
    dims,
    offset_ref, kv_ref, qr_ref, resid_ref, routes_ref, probs_ref,
    q_hbm, wuv_hbm, wout_hbm, wg_hbm, wu_hbm, wd_hbm,
    attn_ref, mix_ref,
    q_buf, wuv, wout, wg, wu, wd,
    kx, tool_buf, keys, wts, allv, oacc,
    p1, rc1, q1, ry1, xg, p2, rc2, q2, ry2, t2, rz2,
    q_sem, w_sem,
    kz_s, ky_s, kc_s, k_r,
    wt_s, wt_r,
    v_s, v_r,
    o_s, oc_r, oy_r,
    xz_s, xy_s, xc_s, x_r,
    pc_s, pc_r, py_s, py_r, pz_s, pz_r,
):
    S, E, G, ctx_dev, tool_dev = dims
    Y = E // 2
    heads, T, LAT = q_buf.shape
    VD = wuv.shape[2]
    n = heads // G
    GV = G * VD
    TOK, C = resid_ref.shape
    ctx, tool_len = S * ctx_dev, S * tool_dev
    suf = S * T
    rope = qr_ref.shape[1] // heads
    s = lax.axis_index("seq")
    e = lax.axis_index("expert")
    y, c = lax.div(e, 2), lax.rem(e, 2)
    sister = e + 1 - 2 * c

    def seq_at(d):
        return lax.rem(s + d, S)

    def y_at(d):
        return lax.rem(y + d, Y)

    pending = []

    def send(src, dst, send_sem, recv_sem, **where):
        copy = pltpu.make_async_remote_copy(
            src_ref=src, dst_ref=dst, send_sem=send_sem, recv_sem=recv_sem,
            device_id=where, device_id_type=MESH,
        )
        copy.start()
        return copy

    def arrived(dst, sem):
        pltpu.make_async_remote_copy(
            src_ref=dst, dst_ref=dst, send_sem=sem, recv_sem=sem,
            device_id={"expert": sister}, device_id_type=MESH,
        ).wait_recv()

    barrier = pltpu.get_barrier_semaphore()
    for d in range(1, S):
        pl.semaphore_signal(barrier, inc=1, device_id={"seq": seq_at(d)}, device_id_type=MESH)
    for d in range(1, E):
        pl.semaphore_signal(
            barrier, inc=1, device_id={"expert": lax.rem(e + d, E)}, device_id_type=MESH
        )

    def q_copy(h):
        return pltpu.make_async_copy(
            q_hbm.at[:, pl.ds(pl.multiple_of(h * LAT, LAT), LAT)], q_buf.at[h], q_sem.at[h]
        )

    def start_q(h, carry):
        q_copy(h).start()
        return carry

    loads = [
        pltpu.make_async_copy(a, b, w_sem.at[i])
        for i, (a, b) in enumerate(
            ((wuv_hbm, wuv), (wout_hbm, wout), (wg_hbm.at[0], wg), (wu_hbm.at[0], wu), (wd_hbm.at[0], wd))
        )
    ]
    kx[s, e] = kv_ref[...]
    lane_tok = lax.broadcasted_iota(jnp.int32, (TOK, lanes), 1)
    routes = routes_ref[...]
    probs = probs_ref[...]
    weight = 2.5 * probs / jnp.sum(probs, axis=1, keepdims=True)
    mine = jnp.zeros((TOK, lanes), jnp.float32)
    for k in range(routes.shape[1]):
        mine = mine + jnp.where(routes[:, k : k + 1] == lane_tok, weight[:, k : k + 1], 0.0)
    wts[e] = mine

    pl.semaphore_wait(barrier, S - 1 + E - 1)

    def gather_start(buf, zs, rs):
        for d in range(1, S):
            pending.append(send(buf.at[s, e], buf.at[s, e], zs.at[d], rs.at[s, e], seq=seq_at(d)))

    def gather_forward(buf, ys, cs, rs):
        for i in range(S):
            so = seq_at(i)
            if i > 0:
                arrived(buf.at[so, e], rs.at[so, e])
            for d in range(1, Y):
                pending.append(
                    send(buf.at[so, e], buf.at[so, e], ys.at[i, d], rs.at[so, e], expert=y_at(d) * 2 + c)
                )
            pending.append(send(buf.at[so, e], buf.at[so, e], cs.at[i, 0], rs.at[so, e], expert=sister))
        for i in range(S):
            so = seq_at(i)
            for d in range(1, Y):
                eo = y_at(d) * 2 + c
                arrived(buf.at[so, eo], rs.at[so, eo])
                pending.append(
                    send(buf.at[so, eo], buf.at[so, eo], cs.at[i, d], rs.at[so, eo], expert=sister)
                )

    def gather_end(buf, rs, i):
        so = seq_at(i)
        for d in range(Y):
            eo = y_at(d) * 2 + 1 - c
            arrived(buf.at[so, eo], rs.at[so, eo])

    gather_start(kx, kz_s, k_r)
    for d in range(1, E):
        pending.append(
            send(wts.at[e], wts.at[e], wt_s.at[d], wt_r.at[e], expert=lax.rem(e + d, E))
        )
    lax.fori_loop(0, heads, start_q, 0)
    for load in loads:
        load.start()
    gather_forward(kx, ky_s, kc_s, k_r)
    for i in range(S):
        gather_end(kx, k_r, i)

    width = kx.shape[3]
    for so in range(S):
        block = kx[so].reshape(E * kx.shape[2], width)
        tool_buf[so * tool_dev : (so + 1) * tool_dev] = block[ctx_dev + T : ctx_dev + T + tool_dev]
        keys[ctx + so * T : ctx + (so + 1) * T] = block[ctx_dev : ctx_dev + T]
        keys[so * ctx_dev : (so + 1) * ctx_dev] = block[:ctx_dev]
    offset = offset_ref[0]
    tool_all = tool_buf[...]
    for so in range(S):
        rows = slice(so * ctx_dev, (so + 1) * ctx_dev)
        shifted = so * ctx_dev + lax.broadcasted_iota(jnp.int32, (ctx_dev, tool_len), 0) - offset
        column = lax.broadcasted_iota(jnp.int32, (ctx_dev, tool_len), 1)
        pick = jnp.where(shifted == column, 1.0, 0.0).astype(jnp.bfloat16)
        inside = jnp.sum(pick.astype(jnp.float32), axis=1, keepdims=True) > 0.5
        keys[rows] = jnp.where(
            inside, dot(pick, tool_all), keys[rows].astype(jnp.float32)
        ).astype(jnp.bfloat16)

    def wait_q(h, carry):
        q_copy(h).wait()
        return carry

    lax.fori_loop(0, heads, wait_q, 0)
    loads[0].wait()

    lane_q = lax.broadcasted_iota(jnp.int32, (T, lanes), 1)
    rows_g = G * T
    query_pos = s * T + lax.rem(lax.broadcasted_iota(jnp.int32, (rows_g, suf), 0), T)
    hidden = lax.broadcasted_iota(jnp.int32, (rows_g, suf), 1) > query_pos

    def v_copy(k, d):
        return pltpu.make_async_remote_copy(
            src_ref=allv.at[k, s], dst_ref=allv.at[k, s], send_sem=v_s.at[k, d],
            recv_sem=v_r.at[k, s], device_id={"seq": seq_at(d)}, device_id_type=MESH,
        )

    def attend(k, carry):
        q = q_buf[pl.ds(k * G, G)].reshape(rows_g, LAT)
        step = G * rope
        turned = qr_ref[:, pl.ds(pl.multiple_of(k * step, step), step)].astype(jnp.float32)
        parts = []
        for j in range(G):
            low = j * rope % lanes
            at = j * rope // lanes * lanes
            keep = (lane_q >= low) & (lane_q < low + rope)
            parts.append(jnp.where(keep, turned[:, at : at + lanes], 0.0))
        qr = jnp.concatenate(parts, axis=0).astype(jnp.bfloat16)
        s1 = dot_nt(q, keys[:ctx, :LAT]) + dot_nt(qr, keys[:ctx, LAT:])
        s2 = dot_nt(q, keys[ctx:, :LAT]) + dot_nt(qr, keys[ctx:, LAT:])
        s2 = jnp.where(hidden, floor_score, s2)
        top = jnp.maximum(
            jnp.max(s1, axis=1, keepdims=True), jnp.max(s2, axis=1, keepdims=True)
        )
        e1 = jnp.exp2((s1 - top) * exp2_scale)
        e2 = jnp.exp2((s2 - top) * exp2_scale)
        total = jnp.sum(e1, axis=1, keepdims=True) + jnp.sum(e2, axis=1, keepdims=True)
        acc = dot(e1.astype(jnp.bfloat16), keys[:ctx, :LAT])
        acc = acc + dot(e2.astype(jnp.bfloat16), keys[ctx:, :LAT])
        out = (acc / total).astype(jnp.bfloat16)
        for j in range(G):
            allv[k, s, :, j * VD : (j + 1) * VD] = dot(
                out[j * T : (j + 1) * T], wuv[k * G + j]
            ).astype(jnp.bfloat16)
        for d in range(1, S):
            v_copy(k, d).start()
        return carry

    lax.fori_loop(0, n, attend, 0)

    loads[1].wait()
    oacc[...] = jnp.zeros_like(oacc)
    tile = column_tile(C)

    def project(k, carry):
        for d in range(1, S):
            so = seq_at(d)
            arrived(allv.at[k, so], v_r.at[k, so])
        values = allv[k].reshape(suf, GV)
        at = pl.ds(pl.multiple_of(k * GV, GV), GV)
        for j in range(0, C, tile):
            oacc[:, j : j + tile] += dot(values, wout[at, j : j + tile])
        return carry

    lax.fori_loop(0, n, project, 0)

    for yy in range(Y):
        for cc in range(2):
            b = yy * 2 + cc
            p1[cc, yy] = oacc[b * TOK : (b + 1) * TOK].astype(jnp.bfloat16)
    pending.append(send(p1.at[1 - c], rc1, o_s.at[0], oc_r, expert=sister))
    arrived(rc1, oc_r)
    for yy in range(Y):
        q1[yy] = (p1[c, yy].astype(jnp.float32) + rc1[yy].astype(jnp.float32)).astype(jnp.bfloat16)
    for d in range(1, Y):
        yo = y_at(d)
        pending.append(send(q1.at[yo], ry1.at[y], o_s.at[d], oy_r.at[y], expert=yo * 2 + c))
    summed = resid_ref[...].astype(jnp.float32) + q1[y].astype(jnp.float32)
    for d in range(1, Y):
        yo = y_at(d)
        arrived(ry1.at[yo], oy_r.at[yo])
        summed = summed + ry1[yo].astype(jnp.float32)
    stream = summed.astype(jnp.bfloat16)
    xg[s, e] = stream
    gather_start(xg, xz_s, x_r)
    attn_ref[...] = stream

    for d in range(1, E):
        eo = lax.rem(e + d, E)
        arrived(wts.at[eo], wt_r.at[eo])
    rows_all = E * TOK
    lane_all = lax.broadcasted_iota(jnp.int32, (rows_all, lanes), 1)
    own_weight = jnp.sum(
        jnp.where(lane_all == e, wts[...].reshape(rows_all, lanes), 0.0), axis=1, keepdims=True
    )
    gather_forward(xg, xy_s, xc_s, x_r)

    loads[2].wait()
    loads[3].wait()
    square = jnp.zeros((rows_all, 1), jnp.float32)
    gate = jnp.zeros((rows_all, wg.shape[1]), jnp.float32)
    upper = jnp.zeros((rows_all, wg.shape[1]), jnp.float32)
    for i in range(S):
        gather_end(xg, x_r, i)
        so = seq_at(i)
        x = xg[so].reshape(rows_all, C)
        at = pl.ds(pl.multiple_of(so * C, C), C)
        wide = x.astype(jnp.float32)
        square = square + jnp.sum(wide * wide, axis=1, keepdims=True)
        gate = gate + dot(x, wg[at, :])
        upper = upper + dot(x, wu[at, :])
    inv = lax.rsqrt(square * (1.0 / (S * C)) + norm_eps)
    gate = gate * inv
    inner = (gate / (1.0 + jnp.exp(-gate)) * (upper * inv) * own_weight).astype(jnp.bfloat16)

    loads[4].wait()
    for i in range(S):
        so = seq_at(i + 1)
        for j in range(0, C, tile):
            part = dot(inner, wd[:, pl.ds(pl.multiple_of(so * C + j, 128), tile)]).astype(jnp.bfloat16)
            for yy in range(Y):
                for cc in range(2):
                    b = yy * 2 + cc
                    p2[so, cc, yy, :, j : j + tile] = part[b * TOK : (b + 1) * TOK]
        pending.append(send(p2.at[so, 1 - c], rc2.at[so], pc_s.at[i], pc_r.at[so], expert=sister))
    for i in range(S):
        so = seq_at(i + 1)
        arrived(rc2.at[so], pc_r.at[so])
        for d in range(1, Y + 1):
            yo = y_at(d)
            q2[so, yo] = (
                p2[so, c, yo].astype(jnp.float32) + rc2[so, yo].astype(jnp.float32)
            ).astype(jnp.bfloat16)
            if d < Y:
                pending.append(
                    send(q2.at[so, yo], ry2.at[so, y], py_s.at[i, d], py_r.at[so, y], expert=yo * 2 + c)
                )
    mixed = None
    for i in range(S):
        so = seq_at(i + 1)
        mixed = q2[so, y].astype(jnp.float32)
        for d in range(1, Y):
            yo = y_at(d)
            arrived(ry2.at[so, yo], py_r.at[so, yo])
            mixed = mixed + ry2[so, yo].astype(jnp.float32)
        if i < S - 1:
            t2[so] = mixed.astype(jnp.bfloat16)
            pending.append(send(t2.at[so], rz2.at[s], pz_s.at[i], pz_r.at[s], seq=so))
    for d in range(1, S):
        so = seq_at(S - d)
        arrived(rz2.at[so], pz_r.at[so])
        mixed = mixed + rz2[so].astype(jnp.float32)
    mix_ref[...] = mixed.astype(jnp.bfloat16)

    for copy in pending:
        copy.wait_send()

    def drain(k, carry):
        for d in range(1, S):
            v_copy(k, d).wait_send()
        return carry

    lax.fori_loop(0, n, drain, 0)


def on_device(
    q_lat, q_rope, cache_lat, cache_rope, tool_lat, tool_rope, offset, suf_lat, suf_rope,
    w_uv, w_out, resid, routes, probs, w_gate, w_up, w_down,
):
    S, E = lax.axis_size("seq"), lax.axis_size("expert")
    Y = E // 2
    T = q_lat.shape[0]
    heads, LAT, VD = w_uv.shape
    rope = cache_rope.shape[1]
    ctx_dev, tool_dev = cache_lat.shape[0], tool_lat.shape[0]
    TOK, C = resid.shape
    G = max(g for g in range(1, heads + 1) if heads % g == 0 and g * T <= max(256, 2 * T) and g * rope % lanes == 0)
    n = heads // G
    F = w_gate.shape[2]
    latents = jnp.concatenate([cache_lat, suf_lat, tool_lat], axis=0)
    turned = jnp.concatenate([cache_rope, suf_rope, tool_rope], axis=0)
    packed = jnp.concatenate([latents] + [turned] * (lanes // rope), axis=1)
    total = packed.shape[0]
    piece = -(-total // (16 * E)) * 16
    packed = jnp.pad(packed, ((0, piece * E - total), (0, 0)))
    own = lax.dynamic_slice_in_dim(packed, lax.axis_index("expert") * piece, piece, axis=0)
    width = packed.shape[1]
    bf, f32 = jnp.bfloat16, jnp.float32
    dma, vmem = pltpu.SemaphoreType.DMA, pltpu.VMEM
    in_vmem = pl.BlockSpec(memory_space=pltpu.VMEM)
    anywhere = pl.BlockSpec(memory_space=pl.ANY)
    scratch = [
        vmem((heads, T, LAT), bf), vmem(w_uv.shape, bf), vmem(w_out.shape, bf),
        vmem(w_gate.shape[1:], bf), vmem(w_up.shape[1:], bf), vmem(w_down.shape[1:], bf),
        vmem((S, E, piece, width), bf), vmem((S * tool_dev, width), bf),
        vmem((S * (ctx_dev + T), width), bf), vmem((E, TOK, lanes), f32),
        vmem((n, S, T, G * VD), bf), vmem((S * T, C), f32),
        vmem((2, Y, TOK, C), bf), vmem((Y, TOK, C), bf), vmem((Y, TOK, C), bf), vmem((Y, TOK, C), bf),
        vmem((S, E, TOK, C), bf),
        vmem((S, 2, Y, TOK, C), bf), vmem((S, Y, TOK, C), bf), vmem((S, Y, TOK, C), bf),
        vmem((S, Y, TOK, C), bf), vmem((S, TOK, C), bf), vmem((S, TOK, C), bf),
        dma((heads,)), dma((5,)),
        dma((S,)), dma((S, Y)), dma((S, Y)), dma((S, E)),
        dma((E,)), dma((E,)),
        dma((n, S)), dma((n, S)),
        dma((Y,)), dma, dma((Y,)),
        dma((S,)), dma((S, Y)), dma((S, Y)), dma((S, E)),
        dma((S,)), dma((S,)), dma((S, Y)), dma((S, Y)), dma((S,)), dma((S,)),
    ]
    return pl.pallas_call(
        functools.partial(layer_kernel, (S, E, G, ctx_dev, tool_dev)),
        out_shape=(jax.ShapeDtypeStruct((TOK, C), bf), jax.ShapeDtypeStruct((TOK, C), bf)),
        in_specs=[pl.BlockSpec(memory_space=pltpu.SMEM)] + [in_vmem] * 5 + [anywhere] * 6,
        out_specs=(in_vmem, in_vmem),
        scratch_shapes=scratch,
        compiler_params=pltpu.CompilerParams(
            collective_id=0, has_side_effects=True, vmem_limit_bytes=61 * 1024 * 1024
        ),
    )(offset, own, q_rope, resid, routes, probs, q_lat, w_uv, w_out, w_gate, w_up, w_down)


def solution(mesh):
    placed = (
        P(("groups", "seq"), "expert"),
        P(("groups", "seq"), "expert"),
        P(("groups", "seq"), None),
        P(("groups", "seq"), None),
        P(("groups", "seq"), None),
        P(("groups", "seq"), None),
        P("groups"),
        P(("groups", "seq"), None),
        P(("groups", "seq"), None),
        P("expert", None, None),
        P("expert", "seq"),
        P(("groups", "expert"), "seq"),
        P(("groups", "expert"), None),
        P(("groups", "expert"), None),
        P("expert", None, "seq"),
        P("expert", None, "seq"),
        P("expert", "seq", None),
    )
    return jax.shard_map(
        on_device,
        mesh=mesh,
        in_specs=placed,
        out_specs=(P(("groups", "expert"), "seq"), P(("groups", "expert"), "seq")),
        check_vma=False,
    )
```

```python
import functools

import jax
import jax.numpy as jnp
from jax import lax
from jax.experimental import pallas as pl
from jax.experimental.pallas import tpu as pltpu
from jax.sharding import PartitionSpec as P

MESH = pl.DeviceIdType.MESH
norm_eps = 1e-06
exp2_scale = 192.0 ** (-0.5) * 1.4426950408889634
floor_score = -1e30
lanes = 128


def dot(a, b):
    return jnp.dot(a, b, preferred_element_type=jnp.float32)


def dot_nt(a, b):
    return lax.dot_general(a, b, (((1,), (1,)), ((), ())), preferred_element_type=jnp.float32)


def column_tile(width):
    return 256 if width % 256 == 0 else 128


def layer_kernel(
    dims,
    offset_ref, kv_ref, qr_ref, resid_ref, routes_ref, probs_ref,
    q_hbm, wuv_hbm, wout_hbm, wg_hbm, wu_hbm, wd_hbm,
    attn_ref, mix_ref,
    q_buf, wuv, wout, wg, wu, wd,
    kx, tool_buf, keys, wts, allv, oacc,
    p1, rc1, q1, ry1, xg, p2, rc2, q2, ry2, t2, rz2,
    q_sem, w_sem,
    kz_s, ky_s, kc_s, k_r,
    wt_s, wt_r,
    v_s, v_r,
    o_s, oc_r, oy_r,
    xz_s, xy_s, xc_s, x_r,
    pc_s, pc_r, py_s, py_r, pz_s, pz_r,
):
    S, E, G, ctx_dev, tool_dev = dims
    Y = E // 2
    heads, T, LAT = q_buf.shape
    VD = wuv.shape[2]
    n = heads // G
    GV = G * VD
    TOK, C = resid_ref.shape
    ctx, tool_len = S * ctx_dev, S * tool_dev
    suf = S * T
    rope = qr_ref.shape[1] // heads
    s = lax.axis_index("seq")
    e = lax.axis_index("expert")
    y, c = lax.div(e, 2), lax.rem(e, 2)
    sister = e + 1 - 2 * c

    def seq_at(d):
        return lax.rem(s + d, S)

    def y_at(d):
        return lax.rem(y + d, Y)

    pending = []

    def send(src, dst, send_sem, recv_sem, **where):
        copy = pltpu.make_async_remote_copy(
            src_ref=src, dst_ref=dst, send_sem=send_sem, recv_sem=recv_sem,
            device_id=where, device_id_type=MESH,
        )
        copy.start()
        return copy.wait_send

    def arrived(dst, sem):
        pltpu.make_async_remote_copy(
            src_ref=dst, dst_ref=dst, send_sem=sem, recv_sem=sem,
            device_id={"expert": sister}, device_id_type=MESH,
        ).wait_recv()

    def left(src, sem):
        pltpu.make_async_remote_copy(
            src_ref=src, dst_ref=src, send_sem=sem, recv_sem=sem,
            device_id={"expert": sister}, device_id_type=MESH,
        ).wait_send()

    barrier = pltpu.get_barrier_semaphore()
    for d in range(1, S):
        pl.semaphore_signal(barrier, inc=1, device_id={"seq": seq_at(d)}, device_id_type=MESH)
    for d in range(1, E):
        pl.semaphore_signal(
            barrier, inc=1, device_id={"expert": lax.rem(e + d, E)}, device_id_type=MESH
        )

    def q_copy(h):
        return pltpu.make_async_copy(
            q_hbm.at[:, pl.ds(pl.multiple_of(h * LAT, LAT), LAT)], q_buf.at[h], q_sem.at[h]
        )

    def start_q(h, carry):
        q_copy(h).start()
        return carry

    loads = [
        pltpu.make_async_copy(a, b, w_sem.at[i])
        for i, (a, b) in enumerate(
            ((wuv_hbm, wuv), (wout_hbm, wout), (wg_hbm.at[0], wg), (wu_hbm.at[0], wu), (wd_hbm.at[0], wd))
        )
    ]
    kx[s] = kv_ref[...]
    lane_tok = lax.broadcasted_iota(jnp.int32, (TOK, lanes), 1)
    routes = routes_ref[...]
    probs = probs_ref[...]
    weight = 2.5 * probs / jnp.sum(probs, axis=1, keepdims=True)
    mine = jnp.zeros((TOK, lanes), jnp.float32)
    for k in range(routes.shape[1]):
        mine = mine + jnp.where(routes[:, k : k + 1] == lane_tok, weight[:, k : k + 1], 0.0)
    wts[e] = mine

    pl.semaphore_wait(barrier, S - 1 + E - 1)

    def line(d):
        return (
            (s >= d, s - d, s + 1 < S, s + 1, 0),
            (s + d < S, s + d, s >= 1, s - 1, 1),
        )

    def send_when(cond, *args, **where):
        @pl.when(cond)
        def _():
            send(*args, **where)

        def finish():
            @pl.when(cond)
            def _():
                pltpu.make_async_remote_copy(
                    src_ref=args[0], dst_ref=args[1], send_sem=args[2], recv_sem=args[3],
                    device_id=where, device_id_type=MESH,
                ).wait_send()

        return finish

    def gather_start(buf, zs, rs):
        own = buf.at[s, e]
        pending.append(send_when(s + 1 < S, own, own, zs.at[s, 0], rs.at[s, e], seq=s + 1))
        pending.append(send_when(s >= 1, own, own, zs.at[s, 1], rs.at[s, e], seq=s - 1))

    def gather_forward(buf, zs, ys, cs, rs, with_own):
        def beside(so):
            block = buf.at[so, e]
            for d in range(1, Y):
                send(block, block, ys.at[so, d], rs.at[so, e], expert=y_at(d) * 2 + c)
            send(block, block, cs.at[so, 0], rs.at[so, e], expert=sister)

        def onward(so):
            for d in range(1, Y):
                eo = y_at(d) * 2 + c
                block = buf.at[so, eo]
                arrived(block, rs.at[so, eo])
                send(block, block, cs.at[so, d], rs.at[so, eo], expert=sister)

        if with_own:
            beside(s)
        for d in range(1, S):
            for here, so, more, target, way in line(d):
                @pl.when(here)
                def _(so=so, more=more, target=target, way=way):
                    block = buf.at[so, e]
                    arrived(block, rs.at[so, e])

                    @pl.when(more)
                    def _():
                        send(block, block, zs.at[so, way], rs.at[so, e], seq=target)

                    beside(so)
        if with_own:
            onward(s)
        for d in range(1, S):
            for here, so, more, target, way in line(d):
                @pl.when(here)
                def _(so=so):
                    onward(so)

        def finish():
            def sent(so):
                block = buf.at[so, e]
                for d in range(1, Y):
                    left(block, ys.at[so, d])
                    left(block, cs.at[so, d])
                left(block, cs.at[so, 0])

            if with_own:
                sent(s)
            for d in range(1, S):
                for here, so, more, target, way in line(d):
                    @pl.when(here)
                    def _(so=so, more=more, way=way):
                        @pl.when(more)
                        def _():
                            left(buf.at[so, e], zs.at[so, way])

                        sent(so)

        pending.append(finish)

    def gather_end(buf, rs, i):
        so = seq_at(i)
        for d in range(Y):
            eo = y_at(d) * 2 + 1 - c
            arrived(buf.at[so, eo], rs.at[so, eo])

    gather_start(kx, kz_s, k_r)
    for d in range(1, E):
        pending.append(
            send(wts.at[e], wts.at[e], wt_s.at[d], wt_r.at[e], expert=lax.rem(e + d, E))
        )
    lax.fori_loop(0, heads, start_q, 0)
    for load in loads:
        load.start()
    gather_forward(kx, kz_s, ky_s, kc_s, k_r, False)
    for i in range(1, S):
        gather_end(kx, k_r, i)

    width = kx.shape[3]
    for so in range(S):
        block = kx[so].reshape(E * kx.shape[2], width)
        tool_buf[so * tool_dev : (so + 1) * tool_dev] = block[ctx_dev + T : ctx_dev + T + tool_dev]
        keys[ctx + so * T : ctx + (so + 1) * T] = block[ctx_dev : ctx_dev + T]
        keys[so * ctx_dev : (so + 1) * ctx_dev] = block[:ctx_dev]
    offset = offset_ref[0]
    tool_all = tool_buf[...]
    for so in range(S):
        rows = slice(so * ctx_dev, (so + 1) * ctx_dev)
        shifted = so * ctx_dev + lax.broadcasted_iota(jnp.int32, (ctx_dev, tool_len), 0) - offset
        column = lax.broadcasted_iota(jnp.int32, (ctx_dev, tool_len), 1)
        pick = jnp.where(shifted == column, 1.0, 0.0).astype(jnp.bfloat16)
        inside = jnp.sum(pick.astype(jnp.float32), axis=1, keepdims=True) > 0.5
        keys[rows] = jnp.where(
            inside, dot(pick, tool_all), keys[rows].astype(jnp.float32)
        ).astype(jnp.bfloat16)

    def wait_q(h, carry):
        q_copy(h).wait()
        return carry

    lax.fori_loop(0, heads, wait_q, 0)
    loads[0].wait()

    lane_q = lax.broadcasted_iota(jnp.int32, (T, lanes), 1)
    rows_g = G * T
    query_pos = s * T + lax.rem(lax.broadcasted_iota(jnp.int32, (rows_g, suf), 0), T)
    hidden = lax.broadcasted_iota(jnp.int32, (rows_g, suf), 1) > query_pos

    def v_copy(k, origin, way, target):
        return pltpu.make_async_remote_copy(
            src_ref=allv.at[k, origin], dst_ref=allv.at[k, origin], send_sem=v_s.at[k, origin, way],
            recv_sem=v_r.at[k, origin], device_id={"seq": target}, device_id_type=MESH,
        )

    def attend(k):
        q = q_buf[pl.ds(k * G, G)].reshape(rows_g, LAT)
        step = G * rope
        turned = qr_ref[:, pl.ds(pl.multiple_of(k * step, step), step)].astype(jnp.float32)
        parts = []
        for j in range(G):
            low = j * rope % lanes
            at = j * rope // lanes * lanes
            keep = (lane_q >= low) & (lane_q < low + rope)
            parts.append(jnp.where(keep, turned[:, at : at + lanes], 0.0))
        qr = jnp.concatenate(parts, axis=0).astype(jnp.bfloat16)
        s1 = dot_nt(q, keys[:ctx, :LAT]) + dot_nt(qr, keys[:ctx, LAT:])
        s2 = dot_nt(q, keys[ctx:, :LAT]) + dot_nt(qr, keys[ctx:, LAT:])
        s2 = jnp.where(hidden, floor_score, s2)
        top = jnp.maximum(
            jnp.max(s1, axis=1, keepdims=True), jnp.max(s2, axis=1, keepdims=True)
        )
        e1 = jnp.exp2((s1 - top) * exp2_scale)
        e2 = jnp.exp2((s2 - top) * exp2_scale)
        total = jnp.sum(e1, axis=1, keepdims=True) + jnp.sum(e2, axis=1, keepdims=True)
        acc = dot(e1.astype(jnp.bfloat16), keys[:ctx, :LAT])
        acc = acc + dot(e2.astype(jnp.bfloat16), keys[ctx:, :LAT])
        out = (acc / total).astype(jnp.bfloat16)
        for j in range(G):
            allv[k, s, :, j * VD : (j + 1) * VD] = dot(
                out[j * T : (j + 1) * T], wuv[k * G + j]
            ).astype(jnp.bfloat16)
        for more, target, way in ((s + 1 < S, s + 1, 0), (s >= 1, s - 1, 1)):
            @pl.when(more)
            def _(target=target, way=way):
                v_copy(k, s, way, target).start()

    tile = column_tile(C)

    def project(k):
        values = allv[k].reshape(suf, GV)
        at = pl.ds(pl.multiple_of(k * GV, GV), GV)
        for j in range(0, C, tile):
            oacc[:, j : j + tile] += dot(values, wout[at, j : j + tile])

    oacc[...] = jnp.zeros_like(oacc)
    loads[1].wait()
    lag = 2

    def turn(k, carry):
        @pl.when(k < n)
        def _():
            attend(k)

        for d in range(1, S):
            at = k - lag * d

            @pl.when((at >= 0) & (at < n))
            def _(at=at, d=d):
                for here, so, more, target, way in line(d):
                    @pl.when(here)
                    def _(so=so, more=more, target=target, way=way):
                        arrived(allv.at[at, so], v_r.at[at, so])

                        @pl.when(more)
                        def _():
                            v_copy(at, so, way, target).start()

        done = k - lag * (S - 1)

        @pl.when(done >= 0)
        def _():
            project(done)

        return carry

    lax.fori_loop(0, n + lag * (S - 1), turn, 0)

    for yy in range(Y):
        for cc in range(2):
            b = yy * 2 + cc
            p1[cc, yy] = oacc[b * TOK : (b + 1) * TOK].astype(jnp.bfloat16)
    pending.append(send(p1.at[1 - c], rc1, o_s.at[0], oc_r, expert=sister))
    arrived(rc1, oc_r)
    for yy in range(Y):
        q1[yy] = (p1[c, yy].astype(jnp.float32) + rc1[yy].astype(jnp.float32)).astype(jnp.bfloat16)
    for d in range(1, Y):
        yo = y_at(d)
        pending.append(send(q1.at[yo], ry1.at[y], o_s.at[d], oy_r.at[y], expert=yo * 2 + c))
    summed = resid_ref[...].astype(jnp.float32) + q1[y].astype(jnp.float32)
    for d in range(1, Y):
        yo = y_at(d)
        arrived(ry1.at[yo], oy_r.at[yo])
        summed = summed + ry1[yo].astype(jnp.float32)
    stream = summed.astype(jnp.bfloat16)
    xg[s, e] = stream
    gather_start(xg, xz_s, x_r)
    attn_ref[...] = stream

    for d in range(1, E):
        eo = lax.rem(e + d, E)
        arrived(wts.at[eo], wt_r.at[eo])
    rows_all = E * TOK
    lane_all = lax.broadcasted_iota(jnp.int32, (rows_all, lanes), 1)
    own_weight = jnp.sum(
        jnp.where(lane_all == e, wts[...].reshape(rows_all, lanes), 0.0), axis=1, keepdims=True
    )
    gather_forward(xg, xz_s, xy_s, xc_s, x_r, True)

    loads[2].wait()
    loads[3].wait()
    square = jnp.zeros((rows_all, 1), jnp.float32)
    gate = jnp.zeros((rows_all, wg.shape[1]), jnp.float32)
    upper = jnp.zeros((rows_all, wg.shape[1]), jnp.float32)
    for i in range(S):
        gather_end(xg, x_r, i)
        so = seq_at(i)
        x = xg[so].reshape(rows_all, C)
        at = pl.ds(pl.multiple_of(so * C, C), C)
        wide = x.astype(jnp.float32)
        square = square + jnp.sum(wide * wide, axis=1, keepdims=True)
        gate = gate + dot(x, wg[at, :])
        upper = upper + dot(x, wu[at, :])
    inv = lax.rsqrt(square * (1.0 / (S * C)) + norm_eps)
    gate = gate * inv
    inner = (gate / (1.0 + jnp.exp(-gate)) * (upper * inv) * own_weight).astype(jnp.bfloat16)

    loads[4].wait()
    for i in range(S):
        so = seq_at(i + 1)
        for j in range(0, C, tile):
            part = dot(inner, wd[:, pl.ds(pl.multiple_of(so * C + j, 128), tile)]).astype(jnp.bfloat16)
            for yy in range(Y):
                for cc in range(2):
                    b = yy * 2 + cc
                    p2[so, cc, yy, :, j : j + tile] = part[b * TOK : (b + 1) * TOK]
        pending.append(send(p2.at[so, 1 - c], rc2.at[so], pc_s.at[i], pc_r.at[so], expert=sister))
    cut = C // 256 * 128
    halves = ((0, cut), (cut, C - cut))
    units = [(i, h) for i in range(S) for h in range(2)]
    last = [None, None]

    def cores_sum(i, h):
        so = seq_at(i + 1)
        cols = pl.ds(*halves[h])
        if h == 0:
            arrived(rc2.at[so], pc_r.at[so])
        for d in range(1, Y + 1):
            yo = y_at(d)
            q2[so, yo, :, cols] = (
                p2[so, c, yo, :, cols].astype(jnp.float32) + rc2[so, yo, :, cols].astype(jnp.float32)
            ).astype(jnp.bfloat16)
            if d < Y:
                pending.append(
                    send(
                        q2.at[so, yo, :, cols], ry2.at[so, y, :, cols],
                        py_s.at[i, d, h], py_r.at[so, y, h], expert=yo * 2 + c,
                    )
                )

    def chips_sum(i, h):
        so = seq_at(i + 1)
        cols = pl.ds(*halves[h])
        total = q2[so, y, :, cols].astype(jnp.float32)
        for d in range(1, Y):
            yo = y_at(d)
            arrived(ry2.at[so, yo, :, cols], py_r.at[so, yo, h])
            total = total + ry2[so, yo, :, cols].astype(jnp.float32)
        if i < S - 1:
            t2[so, :, cols] = total.astype(jnp.bfloat16)
            pending.append(
                send(t2.at[so, :, cols], rz2.at[s, :, cols], pz_s.at[i, h], pz_r.at[s, h], seq=so)
            )
        else:
            last[h] = total

    ahead = 2
    for at, unit in enumerate(units):
        if at >= ahead:
            chips_sum(*units[at - ahead])
        cores_sum(*unit)
    for unit in units[len(units) - ahead :]:
        chips_sum(*unit)
    for h in range(2):
        cols = pl.ds(*halves[h])
        mixed = last[h]
        for d in range(1, S):
            so = seq_at(S - d)
            arrived(rz2.at[so, :, cols], pz_r.at[so, h])
            mixed = mixed + rz2[so, :, cols].astype(jnp.float32)
        mix_ref[:, cols] = mixed.astype(jnp.bfloat16)

    for finish in pending:
        finish()

    def drain(k, carry):
        for d in range(S):
            for here, so, more, target, way in line(d):
                @pl.when(here & more)
                def _(so=so, way=way, target=target):
                    v_copy(k, so, way, target).wait_send()

        return carry

    lax.fori_loop(0, n, drain, 0)


def on_device(
    q_lat, q_rope, cache_lat, cache_rope, tool_lat, tool_rope, offset, suf_lat, suf_rope,
    w_uv, w_out, resid, routes, probs, w_gate, w_up, w_down,
):
    S, E = lax.axis_size("seq"), lax.axis_size("expert")
    Y = E // 2
    T = q_lat.shape[0]
    heads, LAT, VD = w_uv.shape
    rope = cache_rope.shape[1]
    ctx_dev, tool_dev = cache_lat.shape[0], tool_lat.shape[0]
    TOK, C = resid.shape
    G = max(g for g in range(1, heads + 1) if heads % g == 0 and g * T <= max(256, 2 * T) and g * rope % lanes == 0)
    n = heads // G
    F = w_gate.shape[2]
    latents = jnp.concatenate([cache_lat, suf_lat, tool_lat], axis=0)
    turned = jnp.concatenate([cache_rope, suf_rope, tool_rope], axis=0)
    packed = jnp.concatenate([latents] + [turned] * (lanes // rope), axis=1)
    total = packed.shape[0]
    piece = -(-total // (16 * E)) * 16
    packed = jnp.pad(packed, ((0, piece * E - total), (0, 0)))
    width = packed.shape[1]
    own = packed.reshape(E, piece, width)
    bf, f32 = jnp.bfloat16, jnp.float32
    dma, vmem = pltpu.SemaphoreType.DMA, pltpu.VMEM
    in_vmem = pl.BlockSpec(memory_space=pltpu.VMEM)
    anywhere = pl.BlockSpec(memory_space=pl.ANY)
    scratch = [
        vmem((heads, T, LAT), bf), vmem(w_uv.shape, bf), vmem(w_out.shape, bf),
        vmem(w_gate.shape[1:], bf), vmem(w_up.shape[1:], bf), vmem(w_down.shape[1:], bf),
        vmem((S, E, piece, width), bf), vmem((S * tool_dev, width), bf),
        vmem((S * (ctx_dev + T), width), bf), vmem((E, TOK, lanes), f32),
        vmem((n, S, T, G * VD), bf), vmem((S * T, C), f32),
        vmem((2, Y, TOK, C), bf), vmem((Y, TOK, C), bf), vmem((Y, TOK, C), bf), vmem((Y, TOK, C), bf),
        vmem((S, E, TOK, C), bf),
        vmem((S, 2, Y, TOK, C), bf), vmem((S, Y, TOK, C), bf), vmem((S, Y, TOK, C), bf),
        vmem((S, Y, TOK, C), bf), vmem((S, TOK, C), bf), vmem((S, TOK, C), bf),
        dma((heads,)), dma((5,)),
        dma((S, 2)), dma((S, Y)), dma((S, Y)), dma((S, E)),
        dma((E,)), dma((E,)),
        dma((n, S, 2)), dma((n, S)),
        dma((Y,)), dma, dma((Y,)),
        dma((S, 2)), dma((S, Y)), dma((S, Y)), dma((S, E)),
        dma((S,)), dma((S,)), dma((S, Y, 2)), dma((S, Y, 2)), dma((S, 2)), dma((S, 2)),
    ]
    return pl.pallas_call(
        functools.partial(layer_kernel, (S, E, G, ctx_dev, tool_dev)),
        out_shape=(jax.ShapeDtypeStruct((TOK, C), bf), jax.ShapeDtypeStruct((TOK, C), bf)),
        in_specs=[pl.BlockSpec(memory_space=pltpu.SMEM)] + [in_vmem] * 5 + [anywhere] * 6,
        out_specs=(in_vmem, in_vmem),
        scratch_shapes=scratch,
        compiler_params=pltpu.CompilerParams(
            collective_id=0, has_side_effects=True, vmem_limit_bytes=61 * 1024 * 1024
        ),
    )(offset, own, q_rope, resid, routes, probs, q_lat, w_uv, w_out, w_gate, w_up, w_down)


def solution(mesh):
    placed = (
        P(("groups", "seq"), "expert"),
        P(("groups", "seq"), "expert"),
        P(("groups", "seq"), None),
        P(("groups", "seq"), None),
        P(("groups", "seq"), None),
        P(("groups", "seq"), None),
        P("groups"),
        P(("groups", "seq"), None),
        P(("groups", "seq"), None),
        P("expert", None, None),
        P("expert", "seq"),
        P(("groups", "expert"), "seq"),
        P(("groups", "expert"), None),
        P(("groups", "expert"), None),
        P("expert", None, "seq"),
        P("expert", None, "seq"),
        P("expert", "seq", None),
    )
    return jax.shard_map(
        on_device,
        mesh=mesh,
        in_specs=placed,
        out_specs=(P(("groups", "expert"), "seq"), P(("groups", "expert"), "seq")),
        check_vma=False,
    )
```

```python
import functools

import jax
import jax.numpy as jnp
from jax import lax
from jax.experimental import pallas as pl
from jax.experimental.pallas import tpu as pltpu
from jax.sharding import PartitionSpec as P

MESH = pl.DeviceIdType.MESH
norm_eps = 1e-06
exp2_scale = 192.0 ** (-0.5) * 1.4426950408889634
floor_score = -1e30
lanes = 128


def dot(a, b):
    return jnp.dot(a, b, preferred_element_type=jnp.float32)


def dot_nt(a, b):
    return lax.dot_general(a, b, (((1,), (1,)), ((), ())), preferred_element_type=jnp.float32)


def column_tile(width):
    return 256 if width % 256 == 0 else 128


def layer_kernel(
    dims,
    offset_ref, qr_ref, resid_ref, routes_ref, probs_ref,
    cache_ref, cturn_ref, tool_ref, tturn_ref, suf_ref, sturn_ref,
    q_hbm, wuv_hbm, wout_hbm, wg_hbm, wu_hbm, wd_hbm,
    attn_ref, mix_ref,
    q_buf, wuv, wout, wg, wu, wd,
    kx, tool_buf, keys, wts, allv, oacc,
    p1, rc1, q1, ry1, xg, square_acc, gate_acc, upper_acc, p2, rc2, q2, ry2, t2, rz2,
    q_sem, w_sem,
    kz_s, ky_s, kc_s, k_r,
    wt_s, wt_r,
    v_s, v_r,
    o_s, oc_r, oy_r,
    xz_s, xy_s, xc_s, x_r,
    pc_s, pc_r, py_s, py_r, pz_s, pz_r,
):
    S, E, G, ctx_dev, tool_dev = dims
    Y = E // 2
    heads, T, LAT = q_buf.shape
    VD = wuv.shape[2]
    n = heads // G
    GV = G * VD
    TOK, C = resid_ref.shape
    ctx, tool_len = S * ctx_dev, S * tool_dev
    suf = S * T
    rope = qr_ref.shape[1] // heads
    s = lax.axis_index("seq")
    e = lax.axis_index("expert")
    y, c = lax.div(e, 2), lax.rem(e, 2)
    sister = e + 1 - 2 * c

    def seq_at(d):
        return lax.rem(s + d, S)

    def y_at(d):
        return lax.rem(y + d, Y)

    pending = []

    def send(src, dst, send_sem, recv_sem, **where):
        copy = pltpu.make_async_remote_copy(
            src_ref=src, dst_ref=dst, send_sem=send_sem, recv_sem=recv_sem,
            device_id=where, device_id_type=MESH,
        )
        copy.start()
        return copy.wait_send

    def arrived(dst, sem):
        pltpu.make_async_remote_copy(
            src_ref=dst, dst_ref=dst, send_sem=sem, recv_sem=sem,
            device_id={"expert": sister}, device_id_type=MESH,
        ).wait_recv()

    def left(src, sem):
        pltpu.make_async_remote_copy(
            src_ref=src, dst_ref=src, send_sem=sem, recv_sem=sem,
            device_id={"expert": sister}, device_id_type=MESH,
        ).wait_send()

    barrier = pltpu.get_barrier_semaphore()
    for d in range(1, S):
        pl.semaphore_signal(barrier, inc=1, device_id={"seq": seq_at(d)}, device_id_type=MESH)
    for d in range(1, E):
        pl.semaphore_signal(
            barrier, inc=1, device_id={"expert": lax.rem(e + d, E)}, device_id_type=MESH
        )

    def q_copy(h):
        return pltpu.make_async_copy(
            q_hbm.at[:, pl.ds(pl.multiple_of(h * LAT, LAT), LAT)], q_buf.at[h], q_sem.at[h]
        )

    def start_q(h, carry):
        q_copy(h).start()
        return carry

    loads = [
        pltpu.make_async_copy(a, b, w_sem.at[i])
        for i, (a, b) in enumerate(
            ((wuv_hbm, wuv), (wout_hbm, wout), (wg_hbm.at[0], wg), (wu_hbm.at[0], wu), (wd_hbm.at[0], wd))
        )
    ]
    place = jnp.where(
        lax.rem(lax.broadcasted_iota(jnp.int32, (rope, lanes), 1), rope)
        == lax.broadcasted_iota(jnp.int32, (rope, lanes), 0),
        1.0, 0.0,
    ).astype(jnp.bfloat16)
    piece = kx.shape[2]
    first = 0
    for latents, turned in (
        (cache_ref[...], lax.dot_general(
            cturn_ref[...], place, (((0,), (0,)), ((), ())), preferred_element_type=jnp.float32)),
        (suf_ref[...], dot(sturn_ref[...], place)),
        (tool_ref[...], dot(tturn_ref[...], place)),
        (None, None),
    ):
        end = E * piece if latents is None else first + latents.shape[0]
        at = first
        while at < end:
            stop = min(end, (at // piece + 1) * piece)
            rows = slice(at % piece, at % piece + stop - at)
            if latents is None:
                kx[s, at // piece, rows] = jnp.zeros((stop - at, kx.shape[3]), jnp.bfloat16)
            else:
                kx[s, at // piece, rows, :LAT] = latents[at - first : stop - first]
                kx[s, at // piece, rows, LAT:] = turned[at - first : stop - first].astype(jnp.bfloat16)
            at = stop
        first = end
    lane_tok = lax.broadcasted_iota(jnp.int32, (TOK, lanes), 1)
    probs = probs_ref[...]
    weight = 2.5 * probs / jnp.sum(probs, axis=0, keepdims=True)
    routes = routes_ref[...].astype(jnp.float32)
    same = lax.broadcasted_iota(jnp.int32, (TOK, TOK), 0) == lax.broadcasted_iota(
        jnp.int32, (TOK, TOK), 1
    )

    def upright(row):
        return jnp.sum(jnp.where(same, row, 0.0), axis=1, keepdims=True)

    mine = jnp.zeros((TOK, lanes), jnp.float32)
    for k in range(routes.shape[0]):
        mine = mine + jnp.where(
            upright(routes[k : k + 1]) == lane_tok.astype(jnp.float32), upright(weight[k : k + 1]), 0.0
        )
    wts[e] = mine

    pl.semaphore_wait(barrier, S - 1 + E - 1)

    def line(d):
        return (
            (s >= d, s - d, s + 1 < S, s + 1, 0),
            (s + d < S, s + d, s >= 1, s - 1, 1),
        )

    def send_when(cond, *args, **where):
        @pl.when(cond)
        def _():
            send(*args, **where)

        def finish():
            @pl.when(cond)
            def _():
                pltpu.make_async_remote_copy(
                    src_ref=args[0], dst_ref=args[1], send_sem=args[2], recv_sem=args[3],
                    device_id=where, device_id_type=MESH,
                ).wait_send()

        return finish

    def gather_start(buf, zs, rs):
        own = buf.at[s, e]
        pending.append(send_when(s + 1 < S, own, own, zs.at[s, 0], rs.at[s, e], seq=s + 1))
        pending.append(send_when(s >= 1, own, own, zs.at[s, 1], rs.at[s, e], seq=s - 1))

    def gather_forward(buf, zs, ys, cs, rs, with_own, use):
        def beside(so):
            block = buf.at[so, e]
            for d in range(1, Y):
                send(block, block, ys.at[so, d], rs.at[so, e], expert=y_at(d) * 2 + c)
            send(block, block, cs.at[so, 0], rs.at[so, e], expert=sister)

        def onward(so):
            for d in range(1, Y):
                eo = y_at(d) * 2 + c
                block = buf.at[so, eo]
                arrived(block, rs.at[so, eo])
                send(block, block, cs.at[so, d], rs.at[so, eo], expert=sister)

        def over(d, act):
            if d == 0:
                if with_own:
                    act(s, None, None, None)
            elif 0 < d < S:
                for here, so, more, target, way in line(d):
                    @pl.when(here)
                    def _(so=so, more=more, target=target, way=way):
                        act(so, more, target, way)

        def relay(so, more, target, way):
            if more is not None:
                block = buf.at[so, e]
                arrived(block, rs.at[so, e])

                @pl.when(more)
                def _():
                    send(block, block, zs.at[so, way], rs.at[so, e], seq=target)

            beside(so)

        def complete(so, more, target, way):
            for d in range(Y):
                eo = y_at(d) * 2 + 1 - c
                arrived(buf.at[so, eo], rs.at[so, eo])
            use(so)

        for d in range(S + 2):
            over(d, relay)
            over(d - 1, lambda so, *rest: onward(so))
            over(d - 2, complete)

        def finish():
            def sent(so):
                block = buf.at[so, e]
                for d in range(1, Y):
                    left(block, ys.at[so, d])
                    left(block, cs.at[so, d])
                left(block, cs.at[so, 0])

            if with_own:
                sent(s)
            for d in range(1, S):
                for here, so, more, target, way in line(d):
                    @pl.when(here)
                    def _(so=so, more=more, way=way):
                        @pl.when(more)
                        def _():
                            left(buf.at[so, e], zs.at[so, way])

                        sent(so)

        pending.append(finish)

    gather_start(kx, kz_s, k_r)
    for d in range(1, E):
        pending.append(
            send(wts.at[e], wts.at[e], wt_s.at[d], wt_r.at[e], expert=lax.rem(e + d, E))
        )
    lax.fori_loop(0, heads, start_q, 0)
    for load in loads:
        load.start()
    gather_forward(kx, kz_s, ky_s, kc_s, k_r, False, lambda so: None)

    width = kx.shape[3]
    for so in range(S):
        block = kx[so].reshape(E * kx.shape[2], width)
        tool_buf[so * tool_dev : (so + 1) * tool_dev] = block[ctx_dev + T : ctx_dev + T + tool_dev]
        keys[ctx + so * T : ctx + (so + 1) * T] = block[ctx_dev : ctx_dev + T]
        keys[so * ctx_dev : (so + 1) * ctx_dev] = block[:ctx_dev]
    offset = offset_ref[0]
    tool_all = tool_buf[...]
    for so in range(S):
        rows = slice(so * ctx_dev, (so + 1) * ctx_dev)
        shifted = so * ctx_dev + lax.broadcasted_iota(jnp.int32, (ctx_dev, tool_len), 0) - offset
        column = lax.broadcasted_iota(jnp.int32, (ctx_dev, tool_len), 1)
        pick = jnp.where(shifted == column, 1.0, 0.0).astype(jnp.bfloat16)
        inside = jnp.sum(pick.astype(jnp.float32), axis=1, keepdims=True) > 0.5
        keys[rows] = jnp.where(
            inside, dot(pick, tool_all), keys[rows].astype(jnp.float32)
        ).astype(jnp.bfloat16)

    def wait_q(h, carry):
        q_copy(h).wait()
        return carry

    lax.fori_loop(0, heads, wait_q, 0)
    loads[0].wait()

    lane_q = lax.broadcasted_iota(jnp.int32, (T, lanes), 1)
    rows_g = G * T
    query_pos = s * T + lax.rem(lax.broadcasted_iota(jnp.int32, (rows_g, suf), 0), T)
    hidden = lax.broadcasted_iota(jnp.int32, (rows_g, suf), 1) > query_pos

    def v_copy(k, origin, way, target):
        return pltpu.make_async_remote_copy(
            src_ref=allv.at[k, origin], dst_ref=allv.at[k, origin], send_sem=v_s.at[k, origin, way],
            recv_sem=v_r.at[k, origin], device_id={"seq": target}, device_id_type=MESH,
        )

    def attend(k):
        q = q_buf[pl.ds(k * G, G)].reshape(rows_g, LAT)
        step = G * rope
        turned = qr_ref[:, pl.ds(pl.multiple_of(k * step, step), step)].astype(jnp.float32)
        parts = []
        for j in range(G):
            low = j * rope % lanes
            at = j * rope // lanes * lanes
            keep = (lane_q >= low) & (lane_q < low + rope)
            parts.append(jnp.where(keep, turned[:, at : at + lanes], 0.0))
        qr = jnp.concatenate(parts, axis=0).astype(jnp.bfloat16)
        s1 = dot_nt(q, keys[:ctx, :LAT]) + dot_nt(qr, keys[:ctx, LAT:])
        s2 = dot_nt(q, keys[ctx:, :LAT]) + dot_nt(qr, keys[ctx:, LAT:])
        s2 = jnp.where(hidden, floor_score, s2)
        top = jnp.maximum(
            jnp.max(s1, axis=1, keepdims=True), jnp.max(s2, axis=1, keepdims=True)
        )
        e1 = jnp.exp2((s1 - top) * exp2_scale)
        e2 = jnp.exp2((s2 - top) * exp2_scale)
        total = jnp.sum(e1, axis=1, keepdims=True) + jnp.sum(e2, axis=1, keepdims=True)
        acc = dot(e1.astype(jnp.bfloat16), keys[:ctx, :LAT])
        acc = acc + dot(e2.astype(jnp.bfloat16), keys[ctx:, :LAT])
        out = (acc / total).astype(jnp.bfloat16)
        for j in range(G):
            allv[k, s, :, j * VD : (j + 1) * VD] = dot(
                out[j * T : (j + 1) * T], wuv[k * G + j]
            ).astype(jnp.bfloat16)
        for more, target, way in ((s + 1 < S, s + 1, 0), (s >= 1, s - 1, 1)):
            @pl.when(more)
            def _(target=target, way=way):
                v_copy(k, s, way, target).start()

    tile = column_tile(C)

    def project(k):
        values = allv[k].reshape(suf, GV)
        at = pl.ds(pl.multiple_of(k * GV, GV), GV)
        for j in range(0, C, tile):
            oacc[:, j : j + tile] += dot(values, wout[at, j : j + tile])

    oacc[...] = jnp.zeros_like(oacc)
    loads[1].wait()
    lag = 2

    def turn(k, carry):
        @pl.when(k < n)
        def _():
            attend(k)

        for d in range(1, S):
            at = k - lag * d

            @pl.when((at >= 0) & (at < n))
            def _(at=at, d=d):
                for here, so, more, target, way in line(d):
                    @pl.when(here)
                    def _(so=so, more=more, target=target, way=way):
                        arrived(allv.at[at, so], v_r.at[at, so])

                        @pl.when(more)
                        def _():
                            v_copy(at, so, way, target).start()

        done = k - lag * (S - 1)

        @pl.when(done >= 0)
        def _():
            project(done)

        return carry

    lax.fori_loop(0, n + lag * (S - 1), turn, 0)

    cut = C // 256 * 128
    halves = ((0, cut), (cut, C - cut))
    for h in range(2):
        cols = pl.ds(*halves[h])
        for yy in range(Y):
            for cc in range(2):
                b = yy * 2 + cc
                p1[cc, yy, :, cols] = oacc[b * TOK : (b + 1) * TOK, cols].astype(jnp.bfloat16)
        pending.append(
            send(p1.at[1 - c, :, :, cols], rc1.at[:, :, cols], o_s.at[0, h], oc_r.at[h], expert=sister)
        )
    for h in range(2):
        cols = pl.ds(*halves[h])
        arrived(rc1.at[:, :, cols], oc_r.at[h])
        for d in range(1, Y + 1):
            yo = y_at(d)
            q1[yo, :, cols] = (
                p1[c, yo, :, cols].astype(jnp.float32) + rc1[yo, :, cols].astype(jnp.float32)
            ).astype(jnp.bfloat16)
            if d < Y:
                pending.append(
                    send(
                        q1.at[yo, :, cols], ry1.at[y, :, cols], o_s.at[d, h], oy_r.at[y, h],
                        expert=yo * 2 + c,
                    )
                )
    for h in range(2):
        cols = pl.ds(*halves[h])
        summed = resid_ref[:, cols].astype(jnp.float32) + q1[y, :, cols].astype(jnp.float32)
        for d in range(1, Y):
            yo = y_at(d)
            arrived(ry1.at[yo, :, cols], oy_r.at[yo, h])
            summed = summed + ry1[yo, :, cols].astype(jnp.float32)
        xg[s, e, :, cols] = summed.astype(jnp.bfloat16)
    gather_start(xg, xz_s, x_r)
    attn_ref[...] = xg[s, e]

    for d in range(1, E):
        eo = lax.rem(e + d, E)
        arrived(wts.at[eo], wt_r.at[eo])
    rows_all = E * TOK
    lane_all = lax.broadcasted_iota(jnp.int32, (rows_all, lanes), 1)
    own_weight = jnp.sum(
        jnp.where(lane_all == e, wts[...].reshape(rows_all, lanes), 0.0), axis=1, keepdims=True
    )
    loads[2].wait()
    loads[3].wait()
    square_acc[...] = jnp.zeros_like(square_acc)
    gate_acc[...] = jnp.zeros_like(gate_acc)
    upper_acc[...] = jnp.zeros_like(upper_acc)

    def enter(so):
        x = xg[so].reshape(rows_all, C)
        at = pl.ds(pl.multiple_of(so * C, C), C)
        wide = x.astype(jnp.float32)
        square_acc[...] += jnp.sum(wide * wide, axis=1, keepdims=True)
        gate_acc[...] += dot(x, wg[at, :])
        upper_acc[...] += dot(x, wu[at, :])

    gather_forward(xg, xz_s, xy_s, xc_s, x_r, True, enter)
    square, gate, upper = square_acc[...], gate_acc[...], upper_acc[...]
    inv = lax.rsqrt(square * (1.0 / (S * C)) + norm_eps)
    gate = gate * inv
    inner = (gate / (1.0 + jnp.exp(-gate)) * (upper * inv) * own_weight).astype(jnp.bfloat16)

    loads[4].wait()
    for i in range(S):
        so = seq_at(i + 1)
        for j in range(0, C, tile):
            part = dot(inner, wd[:, pl.ds(pl.multiple_of(so * C + j, 128), tile)]).astype(jnp.bfloat16)
            for yy in range(Y):
                for cc in range(2):
                    b = yy * 2 + cc
                    p2[so, cc, yy, :, j : j + tile] = part[b * TOK : (b + 1) * TOK]
        pending.append(send(p2.at[so, 1 - c], rc2.at[so], pc_s.at[i], pc_r.at[so], expert=sister))
    units = [(i, h) for i in range(S) for h in range(2)]
    last = [None, None]

    def cores_sum(i, h):
        so = seq_at(i + 1)
        cols = pl.ds(*halves[h])
        if h == 0:
            arrived(rc2.at[so], pc_r.at[so])
        for d in range(1, Y + 1):
            yo = y_at(d)
            q2[so, yo, :, cols] = (
                p2[so, c, yo, :, cols].astype(jnp.float32) + rc2[so, yo, :, cols].astype(jnp.float32)
            ).astype(jnp.bfloat16)
            if d < Y:
                pending.append(
                    send(
                        q2.at[so, yo, :, cols], ry2.at[so, y, :, cols],
                        py_s.at[i, d, h], py_r.at[so, y, h], expert=yo * 2 + c,
                    )
                )

    def chips_sum(i, h):
        so = seq_at(i + 1)
        cols = pl.ds(*halves[h])
        total = q2[so, y, :, cols].astype(jnp.float32)
        for d in range(1, Y):
            yo = y_at(d)
            arrived(ry2.at[so, yo, :, cols], py_r.at[so, yo, h])
            total = total + ry2[so, yo, :, cols].astype(jnp.float32)
        if i < S - 1:
            t2[so, :, cols] = total.astype(jnp.bfloat16)
            pending.append(
                send(t2.at[so, :, cols], rz2.at[s, :, cols], pz_s.at[i, h], pz_r.at[s, h], seq=so)
            )
        else:
            last[h] = total

    ahead = 2
    for at, unit in enumerate(units):
        if at >= ahead:
            chips_sum(*units[at - ahead])
        cores_sum(*unit)
    for unit in units[len(units) - ahead :]:
        chips_sum(*unit)
    for h in range(2):
        cols = pl.ds(*halves[h])
        mixed = last[h]
        for d in range(1, S):
            so = seq_at(S - d)
            arrived(rz2.at[so, :, cols], pz_r.at[so, h])
            mixed = mixed + rz2[so, :, cols].astype(jnp.float32)
        mix_ref[:, cols] = mixed.astype(jnp.bfloat16)

    for finish in pending:
        finish()

    def drain(k, carry):
        for d in range(S):
            for here, so, more, target, way in line(d):
                @pl.when(here & more)
                def _(so=so, way=way, target=target):
                    v_copy(k, so, way, target).wait_send()

        return carry

    lax.fori_loop(0, n, drain, 0)


def on_device(
    q_lat, q_rope, cache_lat, cache_rope, tool_lat, tool_rope, offset, suf_lat, suf_rope,
    w_uv, w_out, resid, routes, probs, w_gate, w_up, w_down,
):
    S, E = lax.axis_size("seq"), lax.axis_size("expert")
    Y = E // 2
    T = q_lat.shape[0]
    heads, LAT, VD = w_uv.shape
    rope = cache_rope.shape[1]
    ctx_dev, tool_dev = cache_lat.shape[0], tool_lat.shape[0]
    TOK, C = resid.shape
    G = max(g for g in range(1, heads + 1) if heads % g == 0 and g * T <= max(256, 2 * T) and g * rope % lanes == 0)
    n = heads // G
    F = w_gate.shape[2]
    piece = -(-(ctx_dev + T + tool_dev) // (16 * E)) * 16
    width = LAT + lanes
    bf, f32 = jnp.bfloat16, jnp.float32
    dma, vmem = pltpu.SemaphoreType.DMA, pltpu.VMEM
    in_vmem = pl.BlockSpec(memory_space=pltpu.VMEM)
    anywhere = pl.BlockSpec(memory_space=pl.ANY)
    scratch = [
        vmem((heads, T, LAT), bf), vmem(w_uv.shape, bf), vmem(w_out.shape, bf),
        vmem(w_gate.shape[1:], bf), vmem(w_up.shape[1:], bf), vmem(w_down.shape[1:], bf),
        vmem((S, E, piece, width), bf), vmem((S * tool_dev, width), bf),
        vmem((S * (ctx_dev + T), width), bf), vmem((E, TOK, lanes), f32),
        vmem((n, S, T, G * VD), bf), vmem((S * T, C), f32),
        vmem((2, Y, TOK, C), bf), vmem((Y, TOK, C), bf), vmem((Y, TOK, C), bf), vmem((Y, TOK, C), bf),
        vmem((S, E, TOK, C), bf),
        vmem((E * TOK, 1), f32), vmem((E * TOK, F), f32), vmem((E * TOK, F), f32),
        vmem((S, 2, Y, TOK, C), bf), vmem((S, Y, TOK, C), bf), vmem((S, Y, TOK, C), bf),
        vmem((S, Y, TOK, C), bf), vmem((S, TOK, C), bf), vmem((S, TOK, C), bf),
        dma((heads,)), dma((5,)),
        dma((S, 2)), dma((S, Y)), dma((S, Y)), dma((S, E)),
        dma((E,)), dma((E,)),
        dma((n, S, 2)), dma((n, S)),
        dma((Y, 2)), dma((2,)), dma((Y, 2)),
        dma((S, 2)), dma((S, Y)), dma((S, Y)), dma((S, E)),
        dma((S,)), dma((S,)), dma((S, Y, 2)), dma((S, Y, 2)), dma((S, 2)), dma((S, 2)),
    ]
    return pl.pallas_call(
        functools.partial(layer_kernel, (S, E, G, ctx_dev, tool_dev)),
        out_shape=(jax.ShapeDtypeStruct((TOK, C), bf), jax.ShapeDtypeStruct((TOK, C), bf)),
        in_specs=[pl.BlockSpec(memory_space=pltpu.SMEM)] + [in_vmem] * 10 + [anywhere] * 6,
        out_specs=(in_vmem, in_vmem),
        scratch_shapes=scratch,
        compiler_params=pltpu.CompilerParams(
            collective_id=0, has_side_effects=True, vmem_limit_bytes=61 * 1024 * 1024
        ),
    )(
        offset, q_rope, resid, routes.T, probs.T,
        cache_lat, cache_rope.T, tool_lat, tool_rope, suf_lat, suf_rope,
        q_lat, w_uv, w_out, w_gate, w_up, w_down,
    )


def solution(mesh):
    placed = (
        P(("groups", "seq"), "expert"),
        P(("groups", "seq"), "expert"),
        P(("groups", "seq"), None),
        P(("groups", "seq"), None),
        P(("groups", "seq"), None),
        P(("groups", "seq"), None),
        P("groups"),
        P(("groups", "seq"), None),
        P(("groups", "seq"), None),
        P("expert", None, None),
        P("expert", "seq"),
        P(("groups", "expert"), "seq"),
        P(("groups", "expert"), None),
        P(("groups", "expert"), None),
        P("expert", None, "seq"),
        P("expert", None, "seq"),
        P("expert", "seq", None),
    )
    return jax.shard_map(
        on_device,
        mesh=mesh,
        in_specs=placed,
        out_specs=(P(("groups", "expert"), "seq"), P(("groups", "expert"), "seq")),
        check_vma=False,
    )
```

```python
import functools

import jax
import jax.numpy as jnp
from jax import lax
from jax.experimental import pallas as pl
from jax.experimental.pallas import tpu as pltpu
from jax.sharding import PartitionSpec as P

MESH = pl.DeviceIdType.MESH
norm_eps = 1e-06
exp2_scale = 192.0 ** (-0.5) * 1.4426950408889634
floor_score = -1e30
lanes = 128


def dot(a, b):
    return jnp.dot(a, b, preferred_element_type=jnp.float32)


def dot_nt(a, b):
    return lax.dot_general(a, b, (((1,), (1,)), ((), ())), preferred_element_type=jnp.float32)


def column_tile(width):
    return 256 if width % 256 == 0 else 128


def layer_kernel(
    dims,
    offset_ref, qr_ref, resid_ref, routes_ref, probs_ref,
    cache_ref, cturn_ref, tool_ref, tturn_ref, suf_ref, sturn_ref,
    q_hbm, wuv_hbm, wout_hbm, wg_hbm, wu_hbm, wd_hbm,
    attn_ref, mix_ref,
    q_buf, wuv, wout, wg, wu, wd,
    kx, tool_buf, keys, wts, allv, oacc,
    p1, rc1, q1, ry1, xg, square_acc, gate_acc, upper_acc, p2, rc2, q2, ry2, t2, rz2,
    q_sem, w_sem,
    kz_s, ky_s, kc_s, k_r,
    wt_s, wt_r,
    v_s, v_r,
    o_s, oc_r, oy_r,
    xz_s, xy_s, xc_s, x_r,
    pc_s, pc_r, py_s, py_r, pz_s, pz_r,
):
    S, E, G, ctx_dev, tool_dev = dims
    Y = E // 2
    heads, T, LAT = q_buf.shape
    VD = wuv.shape[2]
    n = heads // G
    GV = G * VD
    TOK, C = resid_ref.shape
    ctx, tool_len = S * ctx_dev, S * tool_dev
    suf = S * T
    rope = qr_ref.shape[1] // heads
    s = lax.axis_index("seq")
    e = lax.axis_index("expert")
    y, c = lax.div(e, 2), lax.rem(e, 2)
    sister = e + 1 - 2 * c

    def seq_at(d):
        return lax.rem(s + d, S)

    def y_at(d):
        return lax.rem(y + d, Y)

    pending = []

    def send(src, dst, send_sem, recv_sem, **where):
        copy = pltpu.make_async_remote_copy(
            src_ref=src, dst_ref=dst, send_sem=send_sem, recv_sem=recv_sem,
            device_id=where, device_id_type=MESH,
        )
        copy.start()
        return copy.wait_send

    def arrived(dst, sem):
        pltpu.make_async_remote_copy(
            src_ref=dst, dst_ref=dst, send_sem=sem, recv_sem=sem,
            device_id={"expert": sister}, device_id_type=MESH,
        ).wait_recv()

    def left(src, sem):
        pltpu.make_async_remote_copy(
            src_ref=src, dst_ref=src, send_sem=sem, recv_sem=sem,
            device_id={"expert": sister}, device_id_type=MESH,
        ).wait_send()

    barrier = pltpu.get_barrier_semaphore()
    for d in range(1, S):
        pl.semaphore_signal(barrier, inc=1, device_id={"seq": seq_at(d)}, device_id_type=MESH)
    for d in range(1, E):
        pl.semaphore_signal(
            barrier, inc=1, device_id={"expert": lax.rem(e + d, E)}, device_id_type=MESH
        )

    def q_copy(h):
        return pltpu.make_async_copy(
            q_hbm.at[:, pl.ds(pl.multiple_of(h * LAT, LAT), LAT)], q_buf.at[h], q_sem.at[h]
        )

    def start_q(h, carry):
        q_copy(h).start()
        return carry

    loads = [
        pltpu.make_async_copy(a, b, w_sem.at[i])
        for i, (a, b) in enumerate(
            ((wuv_hbm, wuv), (wout_hbm, wout), (wg_hbm.at[0], wg), (wu_hbm.at[0], wu), (wd_hbm.at[0], wd))
        )
    ]
    place = jnp.where(
        lax.rem(lax.broadcasted_iota(jnp.int32, (rope, lanes), 1), rope)
        == lax.broadcasted_iota(jnp.int32, (rope, lanes), 0),
        1.0, 0.0,
    ).astype(jnp.bfloat16)
    piece = kx.shape[2]
    first = 0
    for latents, turned in (
        (cache_ref[...], lax.dot_general(
            cturn_ref[...], place, (((0,), (0,)), ((), ())), preferred_element_type=jnp.float32)),
        (suf_ref[...], dot(sturn_ref[...], place)),
        (tool_ref[...], dot(tturn_ref[...], place)),
        (None, None),
    ):
        end = E * piece if latents is None else first + latents.shape[0]
        at = first
        while at < end:
            stop = min(end, (at // piece + 1) * piece)
            rows = slice(at % piece, at % piece + stop - at)
            if latents is None:
                kx[s, at // piece, rows] = jnp.zeros((stop - at, kx.shape[3]), jnp.bfloat16)
            else:
                kx[s, at // piece, rows, :LAT] = latents[at - first : stop - first]
                kx[s, at // piece, rows, LAT:] = turned[at - first : stop - first].astype(jnp.bfloat16)
            at = stop
        first = end
    lane_tok = lax.broadcasted_iota(jnp.int32, (TOK, lanes), 1)
    probs = probs_ref[...]
    weight = 2.5 * probs / jnp.sum(probs, axis=0, keepdims=True)
    routes = routes_ref[...].astype(jnp.float32)
    same = lax.broadcasted_iota(jnp.int32, (TOK, TOK), 0) == lax.broadcasted_iota(
        jnp.int32, (TOK, TOK), 1
    )

    def upright(row):
        return jnp.sum(jnp.where(same, row, 0.0), axis=1, keepdims=True)

    mine = jnp.zeros((TOK, lanes), jnp.float32)
    for k in range(routes.shape[0]):
        mine = mine + jnp.where(
            upright(routes[k : k + 1]) == lane_tok.astype(jnp.float32), upright(weight[k : k + 1]), 0.0
        )
    wts[e] = mine

    pl.semaphore_wait(barrier, S - 1 + E - 1)

    def line(d):
        return (
            (s >= d, s - d, s + 1 < S, s + 1, 0),
            (s + d < S, s + d, s >= 1, s - 1, 1),
        )

    def send_when(cond, *args, **where):
        @pl.when(cond)
        def _():
            send(*args, **where)

        def finish():
            @pl.when(cond)
            def _():
                pltpu.make_async_remote_copy(
                    src_ref=args[0], dst_ref=args[1], send_sem=args[2], recv_sem=args[3],
                    device_id=where, device_id_type=MESH,
                ).wait_send()

        return finish

    def gather_start(buf, zs, rs):
        own = buf.at[s, e]
        pending.append(send_when(s + 1 < S, own, own, zs.at[s, 0], rs.at[s, e], seq=s + 1))
        pending.append(send_when(s >= 1, own, own, zs.at[s, 1], rs.at[s, e], seq=s - 1))

    def gather_forward(buf, zs, ys, cs, rs, with_own, use):
        def beside(so):
            block = buf.at[so, e]
            for d in range(1, Y):
                send(block, block, ys.at[so, d], rs.at[so, e], expert=y_at(d) * 2 + c)
            send(block, block, cs.at[so, 0], rs.at[so, e], expert=sister)

        def onward(so):
            for d in range(1, Y):
                eo = y_at(d) * 2 + c
                block = buf.at[so, eo]
                arrived(block, rs.at[so, eo])
                send(block, block, cs.at[so, d], rs.at[so, eo], expert=sister)

        def over(d, act):
            if d == 0:
                if with_own:
                    act(s, None, None, None)
            elif 0 < d < S:
                for here, so, more, target, way in line(d):
                    @pl.when(here)
                    def _(so=so, more=more, target=target, way=way):
                        act(so, more, target, way)

        def relay(so, more, target, way):
            if more is not None:
                block = buf.at[so, e]
                arrived(block, rs.at[so, e])

                @pl.when(more)
                def _():
                    send(block, block, zs.at[so, way], rs.at[so, e], seq=target)

            beside(so)

        def complete(so, more, target, way):
            for d in range(Y):
                eo = y_at(d) * 2 + 1 - c
                arrived(buf.at[so, eo], rs.at[so, eo])
            use(so)

        for d in range(S + 2):
            over(d, relay)
            over(d - 1, lambda so, *rest: onward(so))
            over(d - 2, complete)

        def finish():
            def sent(so):
                block = buf.at[so, e]
                for d in range(1, Y):
                    left(block, ys.at[so, d])
                    left(block, cs.at[so, d])
                left(block, cs.at[so, 0])

            if with_own:
                sent(s)
            for d in range(1, S):
                for here, so, more, target, way in line(d):
                    @pl.when(here)
                    def _(so=so, more=more, way=way):
                        @pl.when(more)
                        def _():
                            left(buf.at[so, e], zs.at[so, way])

                        sent(so)

        pending.append(finish)

    gather_start(kx, kz_s, k_r)
    for d in range(1, E):
        pending.append(
            send(wts.at[e], wts.at[e], wt_s.at[d], wt_r.at[e], expert=lax.rem(e + d, E))
        )
    lax.fori_loop(0, heads, start_q, 0)
    for load in loads:
        load.start()
    gather_forward(kx, kz_s, ky_s, kc_s, k_r, False, lambda so: None)

    width = kx.shape[3]
    for so in range(S):
        block = kx[so].reshape(E * kx.shape[2], width)
        tool_buf[so * tool_dev : (so + 1) * tool_dev] = block[ctx_dev + T : ctx_dev + T + tool_dev]
        keys[ctx + so * T : ctx + (so + 1) * T] = block[ctx_dev : ctx_dev + T]
        keys[so * ctx_dev : (so + 1) * ctx_dev] = block[:ctx_dev]
    offset = offset_ref[0]
    tool_all = tool_buf[...]
    for so in range(S):
        rows = slice(so * ctx_dev, (so + 1) * ctx_dev)
        shifted = so * ctx_dev + lax.broadcasted_iota(jnp.int32, (ctx_dev, tool_len), 0) - offset
        column = lax.broadcasted_iota(jnp.int32, (ctx_dev, tool_len), 1)
        pick = jnp.where(shifted == column, 1.0, 0.0).astype(jnp.bfloat16)
        inside = jnp.sum(pick.astype(jnp.float32), axis=1, keepdims=True) > 0.5
        keys[rows] = jnp.where(
            inside, dot(pick, tool_all), keys[rows].astype(jnp.float32)
        ).astype(jnp.bfloat16)

    def wait_q(h, carry):
        q_copy(h).wait()
        return carry

    lax.fori_loop(0, heads, wait_q, 0)
    loads[0].wait()

    lane_q = lax.broadcasted_iota(jnp.int32, (T, lanes), 1)
    rows_g = G * T
    query_pos = s * T + lax.rem(lax.broadcasted_iota(jnp.int32, (rows_g, suf), 0), T)
    hidden = lax.broadcasted_iota(jnp.int32, (rows_g, suf), 1) > query_pos

    def v_copy(k, origin, way, target):
        return pltpu.make_async_remote_copy(
            src_ref=allv.at[k, origin], dst_ref=allv.at[k, origin], send_sem=v_s.at[k, origin, way],
            recv_sem=v_r.at[k, origin], device_id={"seq": target}, device_id_type=MESH,
        )

    def attend(k):
        q = q_buf[pl.ds(k * G, G)].reshape(rows_g, LAT)
        step = G * rope
        turned = qr_ref[:, pl.ds(pl.multiple_of(k * step, step), step)].astype(jnp.float32)
        parts = []
        for j in range(G):
            low = j * rope % lanes
            at = j * rope // lanes * lanes
            keep = (lane_q >= low) & (lane_q < low + rope)
            parts.append(jnp.where(keep, turned[:, at : at + lanes], 0.0))
        qr = jnp.concatenate(parts, axis=0).astype(jnp.bfloat16)
        s1 = dot_nt(q, keys[:ctx, :LAT]) + dot_nt(qr, keys[:ctx, LAT:])
        s2 = dot_nt(q, keys[ctx:, :LAT]) + dot_nt(qr, keys[ctx:, LAT:])
        s2 = jnp.where(hidden, floor_score, s2)
        top = jnp.maximum(
            jnp.max(s1, axis=1, keepdims=True), jnp.max(s2, axis=1, keepdims=True)
        )
        e1 = jnp.exp2((s1 - top) * exp2_scale)
        e2 = jnp.exp2((s2 - top) * exp2_scale)
        total = jnp.sum(e1, axis=1, keepdims=True) + jnp.sum(e2, axis=1, keepdims=True)
        acc = dot(e1.astype(jnp.bfloat16), keys[:ctx, :LAT])
        acc = acc + dot(e2.astype(jnp.bfloat16), keys[ctx:, :LAT])
        out = (acc / total).astype(jnp.bfloat16)
        for j in range(G):
            allv[k, s, :, j * VD : (j + 1) * VD] = dot(
                out[j * T : (j + 1) * T], wuv[k * G + j]
            ).astype(jnp.bfloat16)
        for more, target, way in ((s + 1 < S, s + 1, 0), (s >= 1, s - 1, 1)):
            @pl.when(more)
            def _(target=target, way=way):
                v_copy(k, s, way, target).start()

    tile = column_tile(C)

    def project(k):
        values = allv[k].reshape(suf, GV)
        at = pl.ds(pl.multiple_of(k * GV, GV), GV)
        for j in range(0, C, tile):
            oacc[:, j : j + tile] += dot(values, wout[at, j : j + tile])

    oacc[...] = jnp.zeros_like(oacc)
    loads[1].wait()
    lag = 2

    def turn(k, carry):
        for d in range(1, S):
            at = k - lag * d

            @pl.when((at >= 0) & (at < n))
            def _(at=at, d=d):
                for here, so, more, target, way in line(d):
                    @pl.when(here)
                    def _(so=so, more=more, target=target, way=way):
                        arrived(allv.at[at, so], v_r.at[at, so])

                        @pl.when(more)
                        def _():
                            v_copy(at, so, way, target).start()

        @pl.when(k < n)
        def _():
            attend(k)

        done = k - lag * (S - 1)

        @pl.when(done >= 0)
        def _():
            project(done)

        return carry

    lax.fori_loop(0, n + lag * (S - 1), turn, 0)

    cut = C // 256 * 128
    halves = ((0, cut), (cut, C - cut))
    for h in range(2):
        cols = pl.ds(*halves[h])
        for yy in range(Y):
            for cc in range(2):
                b = yy * 2 + cc
                p1[cc, yy, :, cols] = oacc[b * TOK : (b + 1) * TOK, cols].astype(jnp.bfloat16)
        pending.append(
            send(p1.at[1 - c, :, :, cols], rc1.at[:, :, cols], o_s.at[0, h], oc_r.at[h], expert=sister)
        )
    for h in range(2):
        cols = pl.ds(*halves[h])
        arrived(rc1.at[:, :, cols], oc_r.at[h])
        for d in range(1, Y + 1):
            yo = y_at(d)
            q1[yo, :, cols] = (
                p1[c, yo, :, cols].astype(jnp.float32) + rc1[yo, :, cols].astype(jnp.float32)
            ).astype(jnp.bfloat16)
            if d < Y:
                pending.append(
                    send(
                        q1.at[yo, :, cols], ry1.at[y, :, cols], o_s.at[d, h], oy_r.at[y, h],
                        expert=yo * 2 + c,
                    )
                )
    for h in range(2):
        cols = pl.ds(*halves[h])
        summed = resid_ref[:, cols].astype(jnp.float32) + q1[y, :, cols].astype(jnp.float32)
        for d in range(1, Y):
            yo = y_at(d)
            arrived(ry1.at[yo, :, cols], oy_r.at[yo, h])
            summed = summed + ry1[yo, :, cols].astype(jnp.float32)
        xg[s, e, :, cols] = summed.astype(jnp.bfloat16)
    gather_start(xg, xz_s, x_r)
    attn_ref[...] = xg[s, e]

    for d in range(1, E):
        eo = lax.rem(e + d, E)
        arrived(wts.at[eo], wt_r.at[eo])
    rows_all = E * TOK
    lane_all = lax.broadcasted_iota(jnp.int32, (rows_all, lanes), 1)
    own_weight = jnp.sum(
        jnp.where(lane_all == e, wts[...].reshape(rows_all, lanes), 0.0), axis=1, keepdims=True
    )
    loads[2].wait()
    loads[3].wait()
    square_acc[...] = jnp.zeros_like(square_acc)
    gate_acc[...] = jnp.zeros_like(gate_acc)
    upper_acc[...] = jnp.zeros_like(upper_acc)

    def enter(so):
        x = xg[so].reshape(rows_all, C)
        at = pl.ds(pl.multiple_of(so * C, C), C)
        wide = x.astype(jnp.float32)
        square_acc[...] += jnp.sum(wide * wide, axis=1, keepdims=True)
        gate_acc[...] += dot(x, wg[at, :])
        upper_acc[...] += dot(x, wu[at, :])

    gather_forward(xg, xz_s, xy_s, xc_s, x_r, True, enter)
    square, gate, upper = square_acc[...], gate_acc[...], upper_acc[...]
    inv = lax.rsqrt(square * (1.0 / (S * C)) + norm_eps)
    gate = gate * inv
    inner = (gate / (1.0 + jnp.exp(-gate)) * (upper * inv) * own_weight).astype(jnp.bfloat16)

    loads[4].wait()

    def produce(i):
        so = seq_at(i + 1)
        for j in range(0, C, tile):
            part = dot(inner, wd[:, pl.ds(pl.multiple_of(so * C + j, 128), tile)]).astype(jnp.bfloat16)
            for yy in range(Y):
                for cc in range(2):
                    b = yy * 2 + cc
                    p2[so, cc, yy, :, j : j + tile] = part[b * TOK : (b + 1) * TOK]
        pending.append(send(p2.at[so, 1 - c], rc2.at[so], pc_s.at[i], pc_r.at[so], expert=sister))
    units = [(i, h) for i in range(S) for h in range(2)]
    last = [None, None]

    def cores_sum(i, h):
        so = seq_at(i + 1)
        cols = pl.ds(*halves[h])
        if h == 0:
            arrived(rc2.at[so], pc_r.at[so])
        for d in range(1, Y + 1):
            yo = y_at(d)
            q2[so, yo, :, cols] = (
                p2[so, c, yo, :, cols].astype(jnp.float32) + rc2[so, yo, :, cols].astype(jnp.float32)
            ).astype(jnp.bfloat16)
            if d < Y:
                pending.append(
                    send(
                        q2.at[so, yo, :, cols], ry2.at[so, y, :, cols],
                        py_s.at[i, d, h], py_r.at[so, y, h], expert=yo * 2 + c,
                    )
                )

    def chips_sum(i, h):
        so = seq_at(i + 1)
        cols = pl.ds(*halves[h])
        total = q2[so, y, :, cols].astype(jnp.float32)
        for d in range(1, Y):
            yo = y_at(d)
            arrived(ry2.at[so, yo, :, cols], py_r.at[so, yo, h])
            total = total + ry2[so, yo, :, cols].astype(jnp.float32)
        if i < S - 1:
            t2[so, :, cols] = total.astype(jnp.bfloat16)
            pending.append(
                send(t2.at[so, :, cols], rz2.at[s, :, cols], pz_s.at[i, h], pz_r.at[s, h], seq=so)
            )
        else:
            last[h] = total

    ahead = 2
    produce(0)
    for at, unit in enumerate(units):
        if unit[1] == 0 and unit[0] + 1 < S:
            produce(unit[0] + 1)
        if at >= ahead:
            chips_sum(*units[at - ahead])
        cores_sum(*unit)
    for unit in units[len(units) - ahead :]:
        chips_sum(*unit)
    for h in range(2):
        cols = pl.ds(*halves[h])
        mixed = last[h]
        for d in range(1, S):
            so = seq_at(S - d)
            arrived(rz2.at[so, :, cols], pz_r.at[so, h])
            mixed = mixed + rz2[so, :, cols].astype(jnp.float32)
        mix_ref[:, cols] = mixed.astype(jnp.bfloat16)

    for finish in pending:
        finish()

    def drain(k, carry):
        for d in range(S):
            for here, so, more, target, way in line(d):
                @pl.when(here & more)
                def _(so=so, way=way, target=target):
                    v_copy(k, so, way, target).wait_send()

        return carry

    lax.fori_loop(0, n, drain, 0)


def on_device(
    q_lat, q_rope, cache_lat, cache_rope, tool_lat, tool_rope, offset, suf_lat, suf_rope,
    w_uv, w_out, resid, routes, probs, w_gate, w_up, w_down,
):
    S, E = lax.axis_size("seq"), lax.axis_size("expert")
    Y = E // 2
    T = q_lat.shape[0]
    heads, LAT, VD = w_uv.shape
    rope = cache_rope.shape[1]
    ctx_dev, tool_dev = cache_lat.shape[0], tool_lat.shape[0]
    TOK, C = resid.shape
    G = max(g for g in range(1, heads + 1) if heads % g == 0 and g * T <= max(256, 2 * T) and g * rope % lanes == 0)
    n = heads // G
    F = w_gate.shape[2]
    piece = -(-(ctx_dev + T + tool_dev) // (16 * E)) * 16
    width = LAT + lanes
    bf, f32 = jnp.bfloat16, jnp.float32
    dma, vmem = pltpu.SemaphoreType.DMA, pltpu.VMEM
    in_vmem = pl.BlockSpec(memory_space=pltpu.VMEM)
    anywhere = pl.BlockSpec(memory_space=pl.ANY)
    scratch = [
        vmem((heads, T, LAT), bf), vmem(w_uv.shape, bf), vmem(w_out.shape, bf),
        vmem(w_gate.shape[1:], bf), vmem(w_up.shape[1:], bf), vmem(w_down.shape[1:], bf),
        vmem((S, E, piece, width), bf), vmem((S * tool_dev, width), bf),
        vmem((S * (ctx_dev + T), width), bf), vmem((E, TOK, lanes), f32),
        vmem((n, S, T, G * VD), bf), vmem((S * T, C), f32),
        vmem((2, Y, TOK, C), bf), vmem((Y, TOK, C), bf), vmem((Y, TOK, C), bf), vmem((Y, TOK, C), bf),
        vmem((S, E, TOK, C), bf),
        vmem((E * TOK, 1), f32), vmem((E * TOK, F), f32), vmem((E * TOK, F), f32),
        vmem((S, 2, Y, TOK, C), bf), vmem((S, Y, TOK, C), bf), vmem((S, Y, TOK, C), bf),
        vmem((S, Y, TOK, C), bf), vmem((S, TOK, C), bf), vmem((S, TOK, C), bf),
        dma((heads,)), dma((5,)),
        dma((S, 2)), dma((S, Y)), dma((S, Y)), dma((S, E)),
        dma((E,)), dma((E,)),
        dma((n, S, 2)), dma((n, S)),
        dma((Y, 2)), dma((2,)), dma((Y, 2)),
        dma((S, 2)), dma((S, Y)), dma((S, Y)), dma((S, E)),
        dma((S,)), dma((S,)), dma((S, Y, 2)), dma((S, Y, 2)), dma((S, 2)), dma((S, 2)),
    ]
    return pl.pallas_call(
        functools.partial(layer_kernel, (S, E, G, ctx_dev, tool_dev)),
        out_shape=(jax.ShapeDtypeStruct((TOK, C), bf), jax.ShapeDtypeStruct((TOK, C), bf)),
        in_specs=[pl.BlockSpec(memory_space=pltpu.SMEM)] + [in_vmem] * 10 + [anywhere] * 6,
        out_specs=(in_vmem, in_vmem),
        scratch_shapes=scratch,
        compiler_params=pltpu.CompilerParams(
            collective_id=0, has_side_effects=True, vmem_limit_bytes=61 * 1024 * 1024
        ),
    )(
        offset, q_rope, resid, routes.T, probs.T,
        cache_lat, cache_rope.T, tool_lat, tool_rope, suf_lat, suf_rope,
        q_lat, w_uv, w_out, w_gate, w_up, w_down,
    )


def solution(mesh):
    placed = (
        P(("groups", "seq"), "expert"),
        P(("groups", "seq"), "expert"),
        P(("groups", "seq"), None),
        P(("groups", "seq"), None),
        P(("groups", "seq"), None),
        P(("groups", "seq"), None),
        P("groups"),
        P(("groups", "seq"), None),
        P(("groups", "seq"), None),
        P("expert", None, None),
        P("expert", "seq"),
        P(("groups", "expert"), "seq"),
        P(("groups", "expert"), None),
        P(("groups", "expert"), None),
        P("expert", None, "seq"),
        P("expert", None, "seq"),
        P("expert", "seq", None),
    )
    return jax.shard_map(
        on_device,
        mesh=mesh,
        in_specs=placed,
        out_specs=(P(("groups", "expert"), "seq"), P(("groups", "expert"), "seq")),
        check_vma=False,
    )
```
